128 devices in a mesh: off: 64 (over z, x, y), kx: 2 (over core).
Axes of the slice: x: 4, y: 4, z: 4, core: 2. Of those that a mesh axis runs over, the one named last changes fastest.
Arguments:
- traces: bfloat16 [65536, 1024], P(('off', 'kx')), may hold values from -6 to 6
- trace_offset: int32 [65536], P(('off', 'kx')), may hold values from 0 to 127, as said below
- trace_midpoint: int32 [65536], P(('off', 'kx')), may hold values from 0 to 1023
- trace_count: int32 [128], P(('off', 'kx')), may hold values from 128 to 512, as said below
- continuation_operator: bfloat16 [512, 2, 128, 128], P('off'), may hold values from -0.5 to 0.5
Outputs:
- continued: float32 [2, 512, 1024, 128], P(None, 'off', 'kx')
The draws below stay inside these ranges and needn't reach their ends.
Inputs may be any that keep to these rules, and one draw needn't show every extreme that they name: `trace_offset`: only the first trace_count[d] rows of device d of off+kx are used. Among them at most 8 go to one owner (an offset of one index of off's 2 planes with a midpoint of one index of kx's 512 midpoints); in every draw some device sends 8 to some owner and some owner receives 8 from every device. `trace_count`: some device uses all its rows.
All inputs are finite; a program needn't handle non-finite values.
Results may differ from the reference program's by a relative error of at most 0.014.
Values may be sent and summed in bfloat16 or wider, within the bound.
A program may use at most 192 MiB of HBM per device.

```python
import jax
import jax.numpy as jnp
from jax import lax

NOFF = 128
NM = 1024
NF = 512
CAP = 8
OWNERS = 128
TR_DEV = 512
TRACES = 65536
OFF_DEV = 2
MID_DEV = 512


def route_plan(base_key):
    key_star, key_full, key_base, key_perm, key_order = jax.random.split(base_key, 5)
    star = jax.random.randint(key_star, (), 0, OWNERS)
    full_device = jax.random.randint(key_full, (), 0, OWNERS)
    sources = jnp.arange(OWNERS, dtype=jnp.int32)
    baseline = jax.random.randint(key_base, (OWNERS, OWNERS), CAP // 4, CAP // 2 + 1)
    baseline = jnp.where(sources[:, None] == full_device, CAP // 2, baseline)
    orders = jax.vmap(jax.random.permutation, in_axes=(0, None))(jax.random.split(key_perm, OWNERS), OWNERS).astype(jnp.int32)
    where_star = jnp.argmax((orders == star).astype(jnp.int32), axis=1)
    leading = orders[:, 0]
    orders = orders.at[sources, where_star].set(leading)
    orders = orders.at[sources, 0].set(jnp.full((OWNERS,), star, jnp.int32))
    heavy = jnp.where(sources % 2 == 0, CAP, 0)
    picked = jnp.take_along_axis(baseline, orders, axis=1)
    values = jnp.where(sources[None, :] < 2 * (OWNERS // 8), heavy[None, :], picked)
    counts = jnp.zeros((OWNERS, OWNERS), jnp.int32).at[sources[:, None], orders].set(values)
    totals = jnp.sum(counts, axis=1).astype(jnp.int32)
    bounds = jnp.cumsum(counts, axis=1)
    slot_index = jnp.arange(TR_DEV, dtype=jnp.int32)
    targets = jnp.sum((bounds[:, None, :] <= slot_index[None, :, None]).astype(jnp.int32), axis=2)
    targets = jnp.minimum(targets, OWNERS - 1)
    shuffles = jax.vmap(jax.random.permutation, in_axes=(0, None))(jax.random.split(key_order, OWNERS), TR_DEV).astype(jnp.int32)
    scores = jnp.where(slot_index[None, :] < totals[:, None], shuffles, TR_DEV + slot_index[None, :])
    arrange = jnp.argsort(scores, axis=1, stable=True)
    targets = jnp.take_along_axis(targets, arrange, axis=1)
    return (targets, totals)


def draw_trace_offset(key, part):
    targets, totals = route_plan(key)
    key = jax.random.fold_in(key, 11)
    within = jax.random.randint(key, (OWNERS, TR_DEV), 0, OFF_DEV)
    kx_devices = NM // MID_DEV
    return (targets // kx_devices * OFF_DEV + within).reshape(TRACES).astype(jnp.int32)


def draw_trace_midpoint(key, part):
    targets, totals = route_plan(key)
    key = jax.random.fold_in(key, 12)
    within = jax.random.randint(key, (OWNERS, TR_DEV), 0, MID_DEV)
    kx_devices = NM // MID_DEV
    return (targets % kx_devices * MID_DEV + within).reshape(TRACES).astype(jnp.int32)


def draw_trace_count(key, part):
    targets, totals = route_plan(key)
    return totals.astype(jnp.int32)


def steps_of(rng, extent, cuts, smallest, top_value):
    def one(dim, shards_of):
        heights = jax.random.uniform(jax.random.fold_in(jax.random.fold_in(rng, 6), dim), (shards_of,), jnp.float32, smallest / len(cuts), top_value / len(cuts))
        return jnp.repeat(jnp.exp(heights), extent[dim] // shards_of).reshape((-1,) + (1,) * (len(extent) - dim - 1))

    factor_of = one(*cuts[0])
    for cut in cuts[1:]:
        factor_of = factor_of * one(*cut)
    return factor_of


def bell_draw(own_key, extent, width, limit, shards=(), kind=jnp.bfloat16):
    level = steps_of(own_key, extent, shards, -0.22, 0.18) if shards else 1.0
    drawn = jax.random.normal(own_key, extent, jnp.float32) * width * level
    return jnp.minimum(jnp.maximum(drawn, -limit), limit).astype(kind)


def setup_inputs(seed: int = 0) -> dict:
    keys = jax.random.split(jax.random.key(seed), 6)
    traces = bell_draw(keys[0], (TRACES, 2 * NF), 1.0, 6.0, ((0, 128),))
    trace_offset = draw_trace_offset(jax.random.fold_in(keys[5], 71), 0)
    trace_midpoint = draw_trace_midpoint(jax.random.fold_in(keys[5], 71), 0)
    trace_count = draw_trace_count(jax.random.fold_in(keys[5], 71), 0)
    continuation_operator = bell_draw(keys[4], (NF, 2, NOFF, NOFF), NOFF ** -0.5, 0.5, ((0, 64),))
    return dict(traces=traces, trace_offset=trace_offset, trace_midpoint=trace_midpoint, trace_count=trace_count, continuation_operator=continuation_operator)


def reference(traces, trace_offset, trace_midpoint, trace_count, continuation_operator):
    position = jnp.arange(TRACES, dtype=jnp.int32)
    owner_index = position // TR_DEV
    used = (position % TR_DEV) < trace_count[owner_index]
    weight = used.astype(jnp.float32)
    bin_index = (trace_offset * NM + trace_midpoint).astype(jnp.int32)
    binned = jax.ops.segment_sum(traces.astype(jnp.float32) * weight[:, None], bin_index, num_segments=NOFF * NM)
    fold_count = jax.ops.segment_sum(weight, bin_index, num_segments=NOFF * NM)
    stacked = (binned / jnp.maximum(fold_count, 1.0)[:, None]).astype(jnp.bfloat16)
    stacked = lax.optimization_barrier(stacked).astype(jnp.float32).reshape(NOFF, NM, 2, NF)
    spectrum = jnp.fft.fft(stacked[:, :, 0, :] + 1j * stacked[:, :, 1, :], axis=1)
    real_part = jnp.real(spectrum).astype(jnp.bfloat16)
    imag_part = jnp.imag(spectrum).astype(jnp.bfloat16)
    real_part = lax.optimization_barrier(real_part).astype(jnp.float32)
    imag_part = lax.optimization_barrier(imag_part).astype(jnp.float32)
    operator = continuation_operator.astype(jnp.float32)
    cont_real = jnp.einsum("fpo,okf->fkp", operator[:, 0], real_part) - jnp.einsum("fpo,okf->fkp", operator[:, 1], imag_part)
    cont_imag = jnp.einsum("fpo,okf->fkp", operator[:, 0], imag_part) + jnp.einsum("fpo,okf->fkp", operator[:, 1], real_part)
    return jnp.stack([cont_real, cont_imag], axis=0)
```

```python
import functools

import jax
import jax.numpy as jnp
import numpy as np
from jax import lax
from jax.experimental import pallas as pl
from jax.experimental.pallas import tpu as pltpu
from jax.sharding import PartitionSpec as P

NOFF = 128
NM = 1024
NF = 512
CAP = 8
OFFS = 64
OWNERS = 128
HALF = 64
SLOTS = OWNERS * CAP
BF = jnp.bfloat16
F32 = jnp.float32

VMEM_SPEC = pl.BlockSpec(memory_space=pltpu.VMEM)
ANY_SPEC = pl.BlockSpec(memory_space=pl.ANY)


def nt(a, b):
    return lax.dot_general(a, b, (((1,), (1,)), ((), ())), preferred_element_type=F32)


def wave_tables():
    k = np.arange(512)
    tables = []
    for par in range(2):
        m = np.concatenate(
            [h * 512 + b * 256 + np.arange(128) * 2 + par for h in range(2) for b in range(2)]
        )
        phase = (k[:, None] * m[None, :]) % NM
        angle = phase * (2.0 * np.pi / NM)
        tables.append(np.concatenate([np.cos(angle), np.sin(angle)], axis=1))
    return np.stack(tables).astype(np.float32)


def prep_kernel(slot_ref, traces_ref, out_ref):
    slot = slot_ref[...]
    place = (
        lax.broadcasted_iota(jnp.int32, (SLOTS, 512), 0) == jnp.broadcast_to(slot, (SLOTS, 512))
    ).astype(F32).astype(BF)

    def part(j, _):
        lanes = pl.multiple_of(j * 128, 128)
        res = []
        for ri in range(2):
            cols = traces_ref[:, pl.ds(ri * NF + lanes, 128)]
            res.append(
                lax.dot_general(cols, place, (((0,), (1,)), ((), ())), preferred_element_type=F32)
            )
        for g in range(16):
            block = jnp.concatenate(
                [res[0][g * 8 : g * 8 + 8], res[1][g * 8 : g * 8 + 8]], axis=0
            ).astype(BF)
            out_ref[j * 16 + g, 0] = block[:, :512]
            out_ref[j * 16 + g, 1] = block[:, 512:]
        return 0

    lax.fori_loop(0, 4, part, 0)


def prepare(slot, traces):
    return pl.pallas_call(
        prep_kernel,
        out_shape=jax.ShapeDtypeStruct((OFFS, 2, 16, 512), BF),
        in_specs=[VMEM_SPEC, VMEM_SPEC],
        out_specs=VMEM_SPEC,
        compiler_params=pltpu.CompilerParams(vmem_limit_bytes=48 << 20),
    )(slot, traces)


def regroup(parts):
    lane = lax.broadcasted_iota(jnp.int32, parts[0].shape, 1) // CAP
    parts = list(parts)
    for b in range(4):
        sh = CAP << b
        low = (lane >> b) % 2 == 0
        new = list(parts)
        for i in range(16):
            if (i >> b) & 1 == 0:
                j = i | (1 << b)
                new[i] = jnp.where(low, parts[i], jnp.roll(parts[j], sh, axis=1))
                new[j] = jnp.where(low, jnp.roll(parts[i], -sh, axis=1), parts[j])
        parts = new
    return parts


def bin_kernel(core, rows_ref, meta_ref, table_ref, own_ref, send_ref, y_ref, mm_ref, left_ref, hot_ref, s32_ref, s16_ref):
    def by_owner(i, _):
        sg, col = i // 4, i % 4
        lanes = pl.multiple_of(col * 128, 128)
        got = regroup([rows_ref[s * 8 + sg, :, pl.ds(lanes, 128)] for s in range(16)])
        for w in range(16):
            y_ref[col * 16 + w, :, pl.ds(pl.multiple_of(sg * 128, 128), 128)] = got[w]
        return 0

    lax.fori_loop(0, 32, by_owner, 0)

    def meta_by_owner(col, _):
        lanes = pl.multiple_of(col * 128, 128)
        got = regroup([meta_ref[s, :, pl.ds(lanes, 128)] for s in range(16)])
        for w in range(16):
            mm_ref[col * 16 + w] = got[w].astype(F32)
        return 0

    lax.fori_loop(0, 4, meta_by_owner, 0)

    def one_owner(w, _):
        pair, h = w // 2, w % 2
        meta = mm_ref[w]
        row_id = lax.broadcasted_iota(jnp.int32, (128, 128), 0).astype(F32).astype(BF)
        one = jnp.ones((), BF)
        zero = jnp.zeros((), BF)
        for sg in range(8):
            lanes = slice(sg * 128, sg * 128 + 128)
            combo = jnp.broadcast_to(meta[2 * sg : 2 * sg + 1], (16, 128)).astype(BF)
            low = jnp.broadcast_to(meta[2 * sg + 1 : 2 * sg + 2], (128, 128)).astype(BF)
            data = y_ref[w, :, lanes]
            for q in range(8):
                left_ref[q * 16 : q * 16 + 16, lanes] = jnp.where(
                    combo == jnp.asarray(q, BF), data, zero
                )
            left_ref[128:144, lanes] = jnp.where(combo == row_id[:16], one, zero)
            hot_ref[:, lanes] = jnp.where(low == row_id, one, zero)
        cells = nt(left_ref[...], hot_ref[...])
        fold = jnp.maximum(cells[128:136], 1.0)
        for q in range(8):
            o2, par, b8 = q // 4, (q // 2) % 2, q % 2
            mean = cells[q * 16 : q * 16 + 16] / fold[q : q + 1]
            cells_of = s32_ref.at[par * 4 + h * 2 + b8]
            row = pair * 2 + o2
            cells_of[pl.ds(row, 8, stride=128), :] = mean[:8]
            cells_of[pl.ds(64 + row, 8, stride=128), :] = mean[8:]
        return 0

    lax.fori_loop(0, HALF, one_owner, 0)

    def to_bf16(f, _):
        r0 = pl.multiple_of(f * 128, 128)
        for lb in range(8):
            par, lane0 = lb // 4, (lb % 4) * 128
            re = s32_ref[lb, pl.ds(r0, 64), :].astype(BF)
            im = s32_ref[lb, pl.ds(r0 + 64, 64), :].astype(BF)
            s16_ref[par, pl.ds(r0, 64), lane0 : lane0 + 128] = re
            s16_ref[par, pl.ds(r0 + 64, 64), lane0 : lane0 + 128] = im
            s16_ref[par, pl.ds(r0, 64), 512 + lane0 : 640 + lane0] = im
            s16_ref[par, pl.ds(r0 + 64, 64), 512 + lane0 : 640 + lane0] = -re
        return 0

    lax.fori_loop(0, 8, to_bf16, 0)
    sign = (1 - 2 * core).astype(F32)

    def transform(f, _):
        r0 = pl.multiple_of(f * 256, 256)
        even = nt(table_ref[0], s16_ref[0, pl.ds(r0, 256), :])
        odd = nt(table_ref[1], s16_ref[1, pl.ds(r0, 256), :]) * sign
        own_ref[:, pl.ds(r0, 256)] = (even + odd).astype(BF)
        send_ref[:, pl.ds(r0, 256)] = (even - odd).astype(BF)
        return 0

    lax.fori_loop(0, 4, transform, 0)


def bin_and_transform(rows, meta, table):
    half = jax.ShapeDtypeStruct((512, 1024), BF)

    def kernel(*refs):
        bin_kernel(lax.axis_index("kx"), *refs)

    return pl.pallas_call(
        kernel,
        out_shape=(half, half),
        in_specs=[VMEM_SPEC] * 3,
        out_specs=(VMEM_SPEC, VMEM_SPEC),
        scratch_shapes=[
            pltpu.VMEM((HALF, 16, 1024), BF),
            pltpu.VMEM((HALF, 16, 128), F32),
            pltpu.VMEM((144, 1024), BF),
            pltpu.VMEM((128, 1024), BF),
            pltpu.VMEM((8, 1024, 128), F32),
            pltpu.VMEM((2, 1024, 1024), BF),
        ],
        compiler_params=pltpu.CompilerParams(vmem_limit_bytes=56 << 20),
    )(rows, meta, table)


def mix_kernel(first_ref, second_ref, op_ref, out_ref):
    for ri in range(2):
        pass
    z = jnp.concatenate([first_ref[...], second_ref[...]], axis=1)
    res = nt(z, op_ref[0])
    out_ref[0, 0] = res[:, :128]
    out_ref[1, 0] = res[:, 128:]


def mix(first, second, op):
    return pl.pallas_call(
        mix_kernel,
        out_shape=jax.ShapeDtypeStruct((2, 8, 512, 128), F32),
        grid=(8,),
        in_specs=[
            pl.BlockSpec((512, 128), lambda f: (0, f)),
            pl.BlockSpec((512, 128), lambda f: (0, f)),
            pl.BlockSpec((1, 256, 256), lambda f: (f, 0, 0)),
        ],
        out_specs=pl.BlockSpec((2, 1, 512, 128), lambda f: (0, f, 0, 0)),
        compiler_params=pltpu.CompilerParams(vmem_limit_bytes=40 << 20),
    )(first, second, op)


def shards(traces, trace_offset, trace_midpoint, trace_count, operator, table):
    core = lax.axis_index("kx")
    position = jnp.arange(512, dtype=jnp.int32)
    live = position < trace_count[0]
    owner = (trace_offset // 2) * 2 + trace_midpoint // 512
    marked = ((owner[:, None] == jnp.arange(OWNERS)[None, :]) & live[:, None]).astype(jnp.int32)
    rank = jnp.sum(jnp.cumsum(marked, axis=0) * marked, axis=1) - 1
    slot = jnp.where(live, owner * CAP + rank, SLOTS)
    combo = (trace_offset % 2) * 4 + (trace_midpoint % 2) * 2 + (trace_midpoint // 256) % 2
    low = (trace_midpoint % 256) // 2
    fields = jnp.stack([combo, low]).astype(F32)
    hot = (slot[:, None] == jnp.arange(SLOTS)[None, :]).astype(BF)
    coded = jnp.dot(fields.astype(BF), hot, preferred_element_type=F32)
    filled = jnp.sum(hot.astype(F32), axis=0)
    coded = jnp.where(filled > 0, coded, 255.0).astype(BF)

    outgoing = prepare(slot[None, :], traces).reshape(OWNERS, 16, 512)
    meta = lax.all_gather(coded, ("off", "kx"))
    meta = lax.dynamic_slice_in_dim(meta, core * 512, 512, axis=2).reshape(16, 16, 512)
    rows = lax.all_to_all(outgoing, ("off", "kx"), split_axis=0, concat_axis=0, tiled=True)
    own, send = bin_and_transform(rows, meta, table)
    other = lax.ppermute(send, "kx", [(0, 1), (1, 0)])
    first = jnp.where(core == 0, own, other)
    second = jnp.where(core == 0, other, own)

    re, im = operator[:, 0], operator[:, 1]
    op = jnp.stack([jnp.stack([re, -im], axis=2), jnp.stack([im, re], axis=2)], axis=1)
    op = op.reshape(8, 2, 128, 2, 2, HALF).transpose(0, 1, 2, 4, 3, 5).reshape(8, 256, 256)
    return mix(first, second, op)


def solution(mesh):
    def run(traces, trace_offset, trace_midpoint, trace_count, operator):
        table = jnp.asarray(wave_tables(), BF)
        return jax.shard_map(
            shards,
            mesh=mesh,
            in_specs=(
                P(("off", "kx"), None),
                P(("off", "kx")),
                P(("off", "kx")),
                P(("off", "kx")),
                P("off", None, None, None),
                P(),
            ),
            out_specs=P(None, "off", "kx", None),
            check_vma=False,
        )(traces, trace_offset, trace_midpoint, trace_count, operator, table)

    return run
```

```python
import jax
import jax.numpy as jnp
import numpy as np
from jax import lax
from jax.experimental import pallas as pl
from jax.experimental.pallas import tpu as pltpu
from jax.sharding import PartitionSpec as P

NM = 1024
NF = 512
CAP = 8
ROWS = 512
CHIPS = 64
HALF = 64
BF = jnp.bfloat16
F32 = jnp.float32
I32 = jnp.int32
MESH = pl.DeviceIdType.MESH

VMEM_SPEC = pl.BlockSpec(memory_space=pltpu.VMEM)
ANY_SPEC = pl.BlockSpec(memory_space=pl.ANY)


def nt(a, b):
    return lax.dot_general(a, b, (((1,), (1,)), ((), ())), preferred_element_type=F32)


def wave_tables():
    k = np.arange(512)
    tables = []
    for par in range(2):
        m = np.concatenate(
            [h * 512 + b * 256 + np.arange(128) * 2 + par for h in range(2) for b in range(2)]
        )
        angle = (k[:, None] * m[None, :]) % NM * (2.0 * np.pi / NM)
        tables.append(np.concatenate([np.cos(angle), np.sin(angle)], axis=1))
    return np.stack(tables).astype(np.float32)


def shifted(off, r, i):
    z, x, y = off // 16, (off // 4) % 4, off % 4
    dx, dy = i // 4, i % 4
    dz = (r + 8 - dx - dy) % 4
    return ((z + dz) % 4) * 16 + ((x + dx) % 4) * 4 + (y + dy) % 4


def sort_rows(xy, off_ref, mid_ref, cnt_ref, traces_ref, blocks_ref, meta_ref):
    offset, mid = off_ref[...], mid_ref[...]
    t = lax.broadcasted_iota(I32, (1, ROWS), 1)
    live = t < jnp.broadcast_to(cnt_ref[...], (1, ROWS))
    owner = jnp.where(live, (offset // 2) * 2 + mid // 512, 1024)
    key = owner * ROWS + t

    position = jnp.zeros((128, ROWS), I32)
    start = jnp.zeros((128, ROWS), I32)
    for b in range(4):
        lanes = slice(b * 128, b * 128 + 128)
        key_col = jnp.broadcast_to(key[:, lanes], (128, 128)).T[:, :1]
        own_col = jnp.broadcast_to(owner[:, lanes], (128, 128)).T[:, :1]
        position += (key_col < key).astype(I32)
        start += (own_col < owner).astype(I32)
    position = jnp.sum(position, axis=0, keepdims=True)
    rank = position - jnp.sum(start, axis=0, keepdims=True)
    position = jnp.where(live, position, ROWS)
    slot = (owner // 16) * 128 + ((owner % 16 + xy) % 16) * CAP + rank
    slot = jnp.where(live, slot, -1)

    combo = (offset % 2) * 4 + (mid % 2) * 2 + (mid // 256) % 2 + 1
    low = (mid % 256) // 2
    fields = jnp.concatenate(
        [position % 128, low, combo, jnp.zeros((13, ROWS), I32)], axis=0
    ).astype(F32).astype(BF)
    hot = (lax.broadcasted_iota(I32, (1024, ROWS), 0) == slot).astype(F32).astype(BF)
    coded = nt(fields, hot)
    coded = coded[0:1] * 8.0 + coded[1:2] * 1024.0 + coded[2:3] * 131072.0
    coded = jnp.concatenate([coded[:, c * 128 : c * 128 + 128] for c in range(8)], axis=0)
    before = jnp.sum(
        (owner < lax.broadcasted_iota(I32, (8, ROWS), 0) * 16).astype(F32), axis=1, keepdims=True
    ).astype(I32)
    lane = lax.broadcasted_iota(I32, (8, 128), 1)
    part = before // 128 + (lane < before % 128).astype(I32)
    meta_ref[...] = coded.astype(I32) + part

    place = (lax.broadcasted_iota(I32, (ROWS, ROWS), 0) == position).astype(F32).astype(BF)

    def cut(j, _):
        lanes = pl.multiple_of(j * 128, 128)
        both = []
        for ri in range(2):
            cols = traces_ref[:, pl.ds(ri * NF + lanes, 128)]
            both.append(
                lax.dot_general(cols, place, (((0,), (1,)), ((), ())), preferred_element_type=F32)
            )
        for g in range(16):
            blocks_ref[j * 16 + g] = jnp.concatenate(
                [both[0][g * 8 : g * 8 + 8], both[1][g * 8 : g * 8 + 8]], axis=0
            ).astype(BF)
        return 0

    lax.fori_loop(0, 4, cut, 0)


def regroup(parts, lane_group):
    now = [parts[(-u) % 16] for u in range(16)]
    for b in range(4):
        bit = (lane_group >> b) % 2 == 1
        now = [jnp.where(bit, now[(u - (1 << b)) % 16], now[u]) for u in range(16)]
    return now


def main_kernel(
    off_ref, mid_ref, cnt_ref, traces_ref, table_hbm, own_ref, other_ref,
    blocks, meta_out, got, meta, ex, dx, y_ref, mm, left, hot, acc, s32, s16, table, give,
    send_sem, recv_sem, msend_sem, mrecv_sem, local_sem, mx_send, mx_recv, dx_send, dx_recv,
    sp_send, sp_recv, table_sem,
):
    off, core = lax.axis_index("off"), lax.axis_index("kx")
    xy = off % 16
    total = off // 16 + (off // 4) % 4 + off % 4
    me = (total % 4) * 16 + xy
    mate = (off, 1 - core)

    bar = pltpu.get_barrier_semaphore()

    def greet(n, _):
        peer = shifted(off, n // 16, n % 16)
        pl.semaphore_signal(bar, inc=1, device_id=(peer, core), device_id_type=MESH)
        return 0

    lax.fori_loop(1, CHIPS, greet, 0)
    pl.semaphore_signal(bar, inc=1, device_id=mate, device_id_type=MESH)
    load_table = pltpu.make_async_copy(table_hbm, table, table_sem)
    load_table.start()

    sort_rows(xy, off_ref, mid_ref, cnt_ref, traces_ref, blocks, meta_out)

    def meta_slot(which, n):
        return meta.at[pl.ds(pl.multiple_of(which * 512 + n * 8, 8), 8)]

    keep = pltpu.make_async_copy(blocks.at[off], got.at[me], local_sem.at[0])
    keep.start()
    keep_meta = pltpu.make_async_copy(meta_out, meta_slot(0, me), local_sem.at[1])
    keep_meta.start()
    pl.semaphore_wait(bar, CHIPS)

    def send_meta(n, _):
        peer = shifted(off, n // 16, n % 16)
        pltpu.make_async_remote_copy(
            meta_out, meta_slot(0, me), msend_sem, mrecv_sem, device_id=(peer, core), device_id_type=MESH
        ).start()
        return 0

    def send_block(n, _):
        peer = shifted(off, n // 16, n % 16)
        pltpu.make_async_remote_copy(
            blocks.at[peer], got.at[me], send_sem, recv_sem.at[n // 16],
            device_id=(peer, core), device_id_type=MESH,
        ).start()
        return 0

    lax.fori_loop(1, CHIPS, send_meta, 0)
    lax.fori_loop(1, CHIPS, send_block, 0)

    def clear(w, _):
        acc[w] = jnp.zeros((144, 128), F32)
        return 0

    lax.fori_loop(0, HALF, clear, 0)

    keep_meta.wait()
    others = meta.at[pl.ds(0, 63 * 8)]
    pltpu.make_async_remote_copy(others, others, msend_sem, mrecv_sem, device_id=mate, device_id_type=MESH).wait()
    pass_meta = pltpu.make_async_remote_copy(
        meta.at[pl.ds(0, 512)], meta.at[pl.ds(512, 512)], mx_send, mx_recv, device_id=mate, device_id_type=MESH
    )
    pass_meta.start()
    pass_meta.wait()

    group16 = lax.broadcasted_iota(I32, (16, 128), 1) // CAP
    group8 = lax.broadcasted_iota(I32, (8, 128), 1) // CAP

    def meta_by_owner(col, _):
        row = core * 4 + col
        parts = [meta[pl.ds(row + s * 8, 8, stride=128), :] for s in range(16)]
        for w, part in enumerate(regroup(parts, group8)):
            mm[col * 16 + w] = part
        return 0

    lax.fori_loop(0, 4, meta_by_owner, 0)

    def one_round(r, _):
        kind = (total + 4 - r) % 4
        base = kind * 16

        def arrived(n):
            part = got.at[pl.ds(0, n)]
            pltpu.make_async_remote_copy(
                part, part, send_sem, recv_sem.at[r], device_id=mate, device_id_type=MESH
            ).wait_recv()

        @pl.when(r == 0)
        def _():
            keep.wait()
            arrived(15)

        @pl.when(r > 0)
        def _():
            arrived(16)

        def expand(s, _):
            n = base + s
            code = meta[pl.ds(pl.multiple_of(n * 8, 8), 8), :]
            index = (code // 8) % 128
            part = code % 8
            x = [got[n, :, i * 128 : i * 128 + 128].astype(F32) for i in range(4)]
            for c in range(8):
                pick = jnp.broadcast_to(part[c : c + 1], (16, 128))
                src = x[min(c, 3)]
                for i in range(min(c, 3) - 1, -1, -1):
                    src = jnp.where(pick == i, x[i], src)
                at = jnp.broadcast_to(index[c : c + 1], (16, 128))
                out = jnp.take_along_axis(src, at, axis=1, mode="promise_in_bounds")
                ex[r, c // 4, s, :, (c % 4) * 128 : (c % 4) * 128 + 128] = out.astype(BF)
            return 0

        lax.fori_loop(0, 16, expand, 0, unroll=4)
        swap = pltpu.make_async_remote_copy(
            ex.at[r, 1 - core], dx.at[r], dx_send.at[r], dx_recv.at[r], device_id=mate, device_id_type=MESH
        )
        swap.start()

        def by_owner(which, col):
            lanes = pl.ds(pl.multiple_of(col * 128, 128), 128)
            if which == 0:
                parts = [ex[r, core, s, :, lanes] for s in range(16)]
            else:
                parts = [dx[r, s, :, lanes] for s in range(16)]
            for w, part in enumerate(regroup(parts, group16)):
                y_ref[col * 16 + w, :, which * 128 : which * 128 + 128] = part

        def own_cols(col, _):
            by_owner(0, col)
            return 0

        def mate_cols(col, _):
            by_owner(1, col)
            return 0

        lax.fori_loop(0, 4, own_cols, 0)
        swap.wait()
        lax.fori_loop(0, 4, mate_cols, 0)

        def four_owners(w4, _):
            row_id = lax.broadcasted_iota(I32, (128, 128), 0).astype(F32).astype(BF)
            one, zero = jnp.ones((), BF), jnp.zeros((), BF)
            for u in range(4):
                w = w4 * 4 + u
                for which in range(2):
                    lanes = slice(which * 128, which * 128 + 128)
                    code = mm[w, pl.ds(which * 4 + kind, 1), :]
                    combo = (code // 131072).astype(F32)
                    low = ((code // 1024) % 128).astype(F32)
                    combo = jnp.broadcast_to(combo, (16, 128)).astype(BF)
                    low = jnp.broadcast_to(low, (128, 128)).astype(BF)
                    data = y_ref[w, :, lanes]
                    for q in range(8):
                        left[u, q * 16 : q * 16 + 16, lanes] = jnp.where(
                            combo == jnp.asarray(q + 1, BF), data, zero
                        )
                    left[u, 128:144, lanes] = jnp.where(combo == row_id[:16] + one, one, zero)
                    hot[u, :, lanes] = jnp.where(low == row_id, one, zero)
                acc[w] += nt(left[u], hot[u])
            return 0

        lax.fori_loop(0, HALF // 4, four_owners, 0)
        return 0

    lax.fori_loop(0, 4, one_round, 0)
    sent = blocks.at[pl.ds(0, 63)]
    pltpu.make_async_remote_copy(
        sent, sent, send_sem, recv_sem.at[0], device_id=mate, device_id_type=MESH
    ).wait_send()

    def means(w, _):
        pair, h = w // 2, w % 2
        fold = jnp.maximum(acc[w, 128:136], 1.0)
        for q in range(8):
            o2, par, b8 = q // 4, (q // 2) % 2, q % 2
            mean = acc[w, q * 16 : q * 16 + 16] / fold[q : q + 1]
            cells_of = s32.at[par * 4 + h * 2 + b8]
            row = pair * 2 + o2
            cells_of[pl.ds(row, 8, stride=128), :] = mean[:8]
            cells_of[pl.ds(64 + row, 8, stride=128), :] = mean[8:]
        return 0

    lax.fori_loop(0, HALF, means, 0)

    load_table.wait()
    sign = (1 - 2 * core).astype(F32)

    def handing(j):
        lanes = pl.ds(pl.multiple_of(j * 256, 256), 256)
        return pltpu.make_async_remote_copy(
            give.at[:, lanes], other_ref.at[:, lanes], sp_send.at[j], sp_recv.at[j],
            device_id=mate, device_id_type=MESH,
        )

    def transform(j, _):
        for f in range(2):
            r0 = pl.multiple_of(j * 256 + f * 128, 128)
            for lb in range(8):
                par, lane0 = lb // 4, (lb % 4) * 128
                re = s32[lb, pl.ds(r0, 64), :].astype(BF)
                im = s32[lb, pl.ds(r0 + 64, 64), :].astype(BF)
                s16[par, pl.ds(r0, 64), lane0 : lane0 + 128] = re
                s16[par, pl.ds(r0 + 64, 64), lane0 : lane0 + 128] = im
                s16[par, pl.ds(r0, 64), 512 + lane0 : 640 + lane0] = im
                s16[par, pl.ds(r0 + 64, 64), 512 + lane0 : 640 + lane0] = -re
        r0 = pl.multiple_of(j * 256, 256)
        even = nt(table[0], s16[0, pl.ds(r0, 256), :])
        odd = nt(table[1], s16[1, pl.ds(r0, 256), :]) * sign
        own_ref[:, pl.ds(r0, 256)] = (even + odd).astype(BF)
        give[:, pl.ds(r0, 256)] = (even - odd).astype(BF)
        handing(j).start()
        return 0

    lax.fori_loop(0, 4, transform, 0)

    def handed(j, _):
        handing(j).wait()
        return 0

    lax.fori_loop(0, 4, handed, 0)


def spectra(offset, mid, count, traces, table):
    half = jax.ShapeDtypeStruct((512, 1024), BF)
    dma = pltpu.SemaphoreType.DMA
    return pl.pallas_call(
        main_kernel,
        out_shape=(half, half),
        in_specs=[VMEM_SPEC] * 4 + [ANY_SPEC],
        out_specs=(VMEM_SPEC, VMEM_SPEC),
        scratch_shapes=[
            pltpu.VMEM((CHIPS, 16, ROWS), BF),
            pltpu.VMEM((8, 128), I32),
            pltpu.VMEM((CHIPS, 16, ROWS), BF),
            pltpu.VMEM((1024, 128), I32),
            pltpu.VMEM((4, 2, 16, 16, 512), BF),
            pltpu.VMEM((4, 16, 16, 512), BF),
            pltpu.VMEM((HALF, 16, 256), BF),
            pltpu.VMEM((HALF, 8, 128), I32),
            pltpu.VMEM((4, 144, 256), BF),
            pltpu.VMEM((4, 128, 256), BF),
            pltpu.VMEM((HALF, 144, 128), F32),
            pltpu.VMEM((8, 1024, 128), F32),
            pltpu.VMEM((2, 1024, 1024), BF),
            pltpu.VMEM((2, 512, 1024), BF),
            pltpu.VMEM((512, 1024), BF),
            dma, dma((4,)), dma, dma, dma((2,)), dma, dma, dma((4,)), dma((4,)),
            dma((4,)), dma((4,)), dma,
        ],
        compiler_params=pltpu.CompilerParams(
            collective_id=0, has_side_effects=True, vmem_limit_bytes=56 << 20
        ),
    )(offset, mid, count, traces, table)


def mix_kernel(own_ref, other_ref, op_ref, out_ref):
    core = lax.axis_index("kx")
    z = jnp.concatenate([own_ref[...], other_ref[...]], axis=1)
    res = nt(z, op_ref[0])
    out_ref[0, 0] = res[:, :128]
    out_ref[1, 0] = res[:, 128:]


def mix(own, other, op):
    return pl.pallas_call(
        mix_kernel,
        out_shape=jax.ShapeDtypeStruct((2, 8, 512, 128), F32),
        grid=(8,),
        in_specs=[
            pl.BlockSpec((512, 128), lambda f: (0, f)),
            pl.BlockSpec((512, 128), lambda f: (0, f)),
            pl.BlockSpec((1, 256, 256), lambda f: (f, 0, 0)),
        ],
        out_specs=pl.BlockSpec((2, 1, 512, 128), lambda f: (0, f, 0, 0)),
        compiler_params=pltpu.CompilerParams(vmem_limit_bytes=40 << 20),
    )(own, other, op)


def shards(traces, trace_offset, trace_midpoint, trace_count, operator, table):
    core = lax.axis_index("kx")
    own, other = spectra(
        trace_offset[None, :], trace_midpoint[None, :], trace_count[None, :], traces, table
    )
    re, im = operator[:, 0], operator[:, 1]
    op = jnp.stack([jnp.stack([re, -im], axis=2), jnp.stack([im, re], axis=2)], axis=1)
    op = op.reshape(8, 2, 128, 2, 2, HALF).transpose(0, 1, 2, 4, 3, 5)
    op = jnp.where(core == 0, op, op[:, :, :, ::-1]).reshape(8, 256, 256)
    return mix(own, other, op)


def solution(mesh):
    def run(traces, trace_offset, trace_midpoint, trace_count, operator):
        table = jnp.asarray(wave_tables(), BF)
        return jax.shard_map(
            shards,
            mesh=mesh,
            in_specs=(
                P(("off", "kx"), None),
                P(("off", "kx")),
                P(("off", "kx")),
                P(("off", "kx")),
                P("off", None, None, None),
                P(),
            ),
            out_specs=P(None, "off", "kx", None),
            check_vma=False,
        )(traces, trace_offset, trace_midpoint, trace_count, operator, table)

    return run
```

```python
import jax
import jax.numpy as jnp
import numpy as np
from jax import lax
from jax.experimental import pallas as pl
from jax.experimental.pallas import tpu as pltpu
from jax.sharding import PartitionSpec as P

NM = 1024
NF = 512
CAP = 8
ROWS = 512
CHIPS = 64
HALF = 64
UNROLL = 16
AHEAD = 4
FREQS = 4
BF = jnp.bfloat16
F32 = jnp.float32
I32 = jnp.int32
MESH = pl.DeviceIdType.MESH

VMEM_SPEC = pl.BlockSpec(memory_space=pltpu.VMEM)
HBM_SPEC = pl.BlockSpec(memory_space=pltpu.HBM)


def nt(a, b):
    return lax.dot_general(a, b, (((1,), (1,)), ((), ())), preferred_element_type=F32)


def wave_tables():
    k = np.arange(512)
    tables = []
    for par in range(2):
        m = np.concatenate(
            [h * 512 + b * 256 + np.arange(128) * 2 + par for h in range(2) for b in range(2)]
        )
        angle = (k[:, None] * m[None, :]) % NM * (2.0 * np.pi / NM)
        tables.append(np.concatenate([np.cos(angle), np.sin(angle)], axis=1))
    return np.stack(tables).astype(np.float32)


def shifted(off, r, i):
    z, x, y = off // 16, (off // 4) % 4, off % 4
    dx, dy = i // 4, i % 4
    dz = (r + 8 - dx - dy) % 4
    return ((z + dz) % 4) * 16 + ((x + dx) % 4) * 4 + (y + dy) % 4


def sort_rows(xy, off_ref, mid_ref, cnt_ref, traces_ref, blocks_ref, meta_ref):
    offset, mid = off_ref[...], mid_ref[...]
    t = lax.broadcasted_iota(I32, (1, ROWS), 1)
    live = t < jnp.broadcast_to(cnt_ref[...], (1, ROWS))
    owner = jnp.where(live, (offset // 2) * 2 + mid // 512, 1024)
    key = owner * ROWS + t

    position = jnp.zeros((128, ROWS), I32)
    start = jnp.zeros((128, ROWS), I32)
    for b in range(4):
        lanes = slice(b * 128, b * 128 + 128)
        key_col = jnp.broadcast_to(key[:, lanes], (128, 128)).T[:, :1]
        own_col = jnp.broadcast_to(owner[:, lanes], (128, 128)).T[:, :1]
        position += (key_col < key).astype(I32)
        start += (own_col < owner).astype(I32)
    position = jnp.sum(position, axis=0, keepdims=True)
    rank = position - jnp.sum(start, axis=0, keepdims=True)
    position = jnp.where(live, position, ROWS)
    slot = (owner // 16) * 128 + ((owner % 16 + xy) % 16) * CAP + rank
    slot = jnp.where(live, slot, -1)

    combo = (offset % 2) * 4 + (mid % 2) * 2 + (mid // 256) % 2 + 1
    low = (mid % 256) // 2
    fields = jnp.concatenate(
        [position % 128, low, combo, jnp.zeros((13, ROWS), I32)], axis=0
    ).astype(F32).astype(BF)
    hot = (lax.broadcasted_iota(I32, (1024, ROWS), 0) == slot).astype(F32).astype(BF)
    coded = nt(fields, hot)
    coded = coded[0:1] * 8.0 + coded[1:2] * 1024.0 + coded[2:3] * 131072.0
    coded = jnp.concatenate([coded[:, c * 128 : c * 128 + 128] for c in range(8)], axis=0)
    before = jnp.sum(
        (owner < lax.broadcasted_iota(I32, (8, ROWS), 0) * 16).astype(F32), axis=1, keepdims=True
    ).astype(I32)
    lane = lax.broadcasted_iota(I32, (8, 128), 1)
    part = before // 128 + (lane < before % 128).astype(I32)
    meta_ref[...] = coded.astype(I32) + part

    place = (lax.broadcasted_iota(I32, (ROWS, ROWS), 0) == position).astype(F32).astype(BF)

    def cut(j, _):
        lanes = pl.multiple_of(j * 128, 128)
        both = []
        for ri in range(2):
            cols = traces_ref[:, pl.ds(ri * NF + lanes, 128)]
            both.append(
                lax.dot_general(cols, place, (((0,), (1,)), ((), ())), preferred_element_type=F32)
            )
        for g in range(16):
            blocks_ref[j * 16 + g] = jnp.concatenate(
                [both[0][g * 8 : g * 8 + 8], both[1][g * 8 : g * 8 + 8]], axis=0
            ).astype(BF)
        return 0

    lax.fori_loop(0, 4, cut, 0)


def regroup(parts, lane_group):
    now = [parts[(-u) % 16] for u in range(16)]
    for b in range(4):
        bit = (lane_group >> b) % 2 == 1
        now = [jnp.where(bit, now[(u - (1 << b)) % 16], now[u]) for u in range(16)]
    return now


def main_kernel(
    off_hbm, mid_hbm, cnt_hbm, traces_hbm, table_hbm, own_ref, other_ref,
    off_ref, mid_ref, cnt_ref, traces_ref, blocks, meta_out, got, meta, ex, dx, y_ref, mm, acc, s32, s16, table, give, own_part,
    send_sem, recv_sem, msend_sem, mrecv_sem, local_sem, mx_send, mx_recv, dx_send, dx_recv,
    sp_send, sp_recv, load_sem, put_sem,
):
    off, core = lax.axis_index("off"), lax.axis_index("kx")
    xy = off % 16
    total = off // 16 + (off // 4) % 4 + off % 4
    me = (total % 4) * 16 + xy
    mate = (off, 1 - core)

    loads = [
        pltpu.make_async_copy(src, dst, load_sem.at[n])
        for n, (src, dst) in enumerate(
            [(off_hbm, off_ref), (mid_hbm, mid_ref), (cnt_hbm, cnt_ref), (traces_hbm, traces_ref), (table_hbm, table)]
        )
    ]
    for load in loads[:4]:
        load.start()
    bar = pltpu.get_barrier_semaphore()

    def greet(n, _):
        peer = shifted(off, n // 16, n % 16)
        pl.semaphore_signal(bar, inc=1, device_id=(peer, core), device_id_type=MESH)
        return 0

    lax.fori_loop(1, CHIPS, greet, 0)
    pl.semaphore_signal(bar, inc=1, device_id=mate, device_id_type=MESH)
    for load in loads[:4]:
        load.wait()
    loads[4].start()

    sort_rows(xy, off_ref, mid_ref, cnt_ref, traces_ref, blocks, meta_out)

    def meta_slot(which, n):
        return meta.at[pl.ds(pl.multiple_of(which * 512 + n * 8, 8), 8)]

    keep = pltpu.make_async_copy(blocks.at[off], got.at[me], local_sem.at[0])
    keep.start()
    keep_meta = pltpu.make_async_copy(meta_out, meta_slot(0, me), local_sem.at[1])
    keep_meta.start()
    pl.semaphore_wait(bar, CHIPS)

    def send_meta(n, _):
        peer = shifted(off, n // 16, n % 16)
        pltpu.make_async_remote_copy(
            meta_out, meta_slot(0, me), msend_sem, mrecv_sem, device_id=(peer, core), device_id_type=MESH
        ).start()
        return 0

    def send_block(n, _):
        peer = shifted(off, n // 16, n % 16)
        pltpu.make_async_remote_copy(
            blocks.at[peer], got.at[me], send_sem, recv_sem.at[n // 16],
            device_id=(peer, core), device_id_type=MESH,
        ).start()
        return 0

    lax.fori_loop(1, CHIPS, send_meta, 0)
    lax.fori_loop(1, AHEAD * 16, send_block, 0)

    def clear(w, _):
        acc[w] = jnp.zeros((144, 128), F32)
        return 0

    lax.fori_loop(0, HALF, clear, 0)

    keep_meta.wait()
    others = meta.at[pl.ds(0, 63 * 8)]
    pltpu.make_async_remote_copy(others, others, msend_sem, mrecv_sem, device_id=mate, device_id_type=MESH).wait()
    pass_meta = pltpu.make_async_remote_copy(
        meta.at[pl.ds(0, 512)], meta.at[pl.ds(512, 512)], mx_send, mx_recv, device_id=mate, device_id_type=MESH
    )
    pass_meta.start()
    pass_meta.wait()

    group16 = lax.broadcasted_iota(I32, (16, 128), 1) // CAP
    group8 = lax.broadcasted_iota(I32, (8, 128), 1) // CAP

    def meta_by_owner(col, _):
        row = core * 4 + col
        parts = [meta[pl.ds(row + s * 8, 8, stride=128), :] for s in range(16)]
        for w, part in enumerate(regroup(parts, group8)):
            mm[col * 16 + w] = part
        return 0

    lax.fori_loop(0, 4, meta_by_owner, 0)

    def exchange(r):
        return pltpu.make_async_remote_copy(
            ex.at[r, 1 - core], dx.at[r], dx_send.at[r], dx_recv.at[r], device_id=mate, device_id_type=MESH
        )

    def take_in(r):
        base = (total + 4 - r) % 4 * 16

        def arrived(n):
            part = got.at[pl.ds(0, n)]
            pltpu.make_async_remote_copy(
                part, part, send_sem, recv_sem.at[r], device_id=mate, device_id_type=MESH
            ).wait_recv()

        @pl.when(r == 0)
        def _():
            keep.wait()
            arrived(15)

        @pl.when(r > 0)
        def _():
            arrived(16)

        @pl.when(r < 4 - AHEAD)
        def _():
            lax.fori_loop((r + AHEAD) * 16, (r + AHEAD + 1) * 16, send_block, 0)

        def expand(s, _):
            n = base + s
            code = meta[pl.ds(pl.multiple_of(n * 8, 8), 8), :]
            index = (code // 8) % 128
            part = code % 8
            x = [got[n, :, i * 128 : i * 128 + 128].astype(F32) for i in range(4)]
            for c in range(8):
                pick = jnp.broadcast_to(part[c : c + 1], (16, 128))
                src = x[min(c, 3)]
                for i in range(min(c, 3) - 1, -1, -1):
                    src = jnp.where(pick == i, x[i], src)
                at = jnp.broadcast_to(index[c : c + 1], (16, 128))
                out = jnp.take_along_axis(src, at, axis=1, mode="promise_in_bounds")
                ex[r, c // 4, s, :, (c % 4) * 128 : (c % 4) * 128 + 128] = out.astype(BF)
            return 0

        lax.fori_loop(0, 16, expand, 0, unroll=8)
        exchange(r).start()

    def one_round(r, last):
        kind = (total + 4 - r) % 4
        exchange(r).wait()

        def by_owner(which, col):
            lanes = pl.ds(pl.multiple_of(col * 128, 128), 128)
            if which == 0:
                parts = [ex[r, core, s, :, lanes] for s in range(16)]
            else:
                parts = [dx[r, s, :, lanes] for s in range(16)]
            for w, part in enumerate(regroup(parts, group16)):
                y_ref[col * 16 + w, :, which * 128 : which * 128 + 128] = part

        def both_cols(col, _):
            by_owner(0, col)
            by_owner(1, col)
            return 0

        lax.fori_loop(0, 4, both_cols, 0)

        def some_owners(g, _):
            row_id = lax.broadcasted_iota(I32, (128, 128), 0).astype(F32).astype(BF)
            one, zero = jnp.ones((), BF), jnp.zeros((), BF)
            for u in range(UNROLL):
                w = g * UNROLL + u
                left, hot = [], []
                for which in range(2):
                    code = mm[w, pl.ds(which * 4 + kind, 1), :]
                    combo = (code // 131072).astype(F32)
                    low = ((code // 1024) % 128).astype(F32)
                    combo = jnp.broadcast_to(combo, (16, 128)).astype(BF)
                    low = jnp.broadcast_to(low, (128, 128)).astype(BF)
                    data = y_ref[w, :, which * 128 : which * 128 + 128]
                    rows = [jnp.where(combo == jnp.asarray(q + 1, BF), data, zero) for q in range(8)]
                    rows.append(jnp.where(combo == row_id[:16] + one, one, zero))
                    left.append(jnp.concatenate(rows, axis=0))
                    hot.append(jnp.where(low == row_id, one, zero))
                cells = nt(jnp.concatenate(left, axis=1), jnp.concatenate(hot, axis=1))
                if not last:
                    acc[w] += cells
                    continue
                cells = acc[w] + cells
                scale = 1.0 / jnp.maximum(cells[128:136], 1.0)
                for q in range(8):
                    o2, par, b8 = q // 4, (q // 2) % 2, q % 2
                    mean = cells[q * 16 : q * 16 + 16] * scale[q : q + 1]
                    cells_of = s32.at[par * 4 + (u % 2) * 2 + b8]
                    row = g * UNROLL + u // 2 * 2 + o2
                    cells_of[pl.ds(row, 8, stride=128), :] = mean[:8]
                    cells_of[pl.ds(64 + row, 8, stride=128), :] = mean[8:]
            return 0

        lax.fori_loop(0, HALF // UNROLL, some_owners, 0)

    def round_of(r, _):
        take_in(r)
        one_round(r - 1, False)
        return 0

    take_in(jnp.int32(0))
    lax.fori_loop(1, 4, round_of, 0)
    one_round(jnp.int32(3), True)
    sent = blocks.at[pl.ds(0, 63)]
    pltpu.make_async_remote_copy(
        sent, sent, send_sem, recv_sem.at[0], device_id=mate, device_id_type=MESH
    ).wait_send()

    loads[4].wait()
    sign = (1 - 2 * core).astype(F32)

    def handing(j):
        lanes = pl.ds(pl.multiple_of(j * 256, 256), 256)
        return pltpu.make_async_remote_copy(
            give.at[:, lanes], other_ref.at[:, lanes], sp_send.at[j], sp_recv.at[j],
            device_id=mate, device_id_type=MESH,
        )

    def putting(j):
        lanes = pl.ds(pl.multiple_of(j * 256, 256), 256)
        return pltpu.make_async_copy(own_part.at[:, lanes], own_ref.at[:, lanes], put_sem.at[j])

    def transform(j, _):
        for f in range(2):
            r0 = pl.multiple_of(j * 256 + f * 128, 128)
            for lb in range(8):
                par, lane0 = lb // 4, (lb % 4) * 128
                re = s32[lb, pl.ds(r0, 64), :].astype(BF)
                im = s32[lb, pl.ds(r0 + 64, 64), :].astype(BF)
                s16[par, pl.ds(r0, 64), lane0 : lane0 + 128] = re
                s16[par, pl.ds(r0 + 64, 64), lane0 : lane0 + 128] = im
                s16[par, pl.ds(r0, 64), 512 + lane0 : 640 + lane0] = im
                s16[par, pl.ds(r0 + 64, 64), 512 + lane0 : 640 + lane0] = -re
        r0 = pl.multiple_of(j * 256, 256)
        even = nt(table[0], s16[0, pl.ds(r0, 256), :])
        odd = nt(table[1], s16[1, pl.ds(r0, 256), :]) * sign
        own_part[:, pl.ds(r0, 256)] = (even + odd).astype(BF)
        putting(j).start()
        give[:, pl.ds(r0, 256)] = (even - odd).astype(BF)
        handing(j).start()
        return 0

    lax.fori_loop(0, 4, transform, 0)

    def handed(j, _):
        putting(j).wait()
        handing(j).wait()
        return 0

    lax.fori_loop(0, 4, handed, 0)


def spectra(offset, mid, count, traces, table):
    half = jax.ShapeDtypeStruct((512, 1024), BF)
    dma = pltpu.SemaphoreType.DMA
    return pl.pallas_call(
        main_kernel,
        out_shape=(half, half),
        in_specs=[HBM_SPEC] * 5,
        out_specs=(HBM_SPEC, HBM_SPEC),
        scratch_shapes=[
            pltpu.VMEM((1, ROWS), I32),
            pltpu.VMEM((1, ROWS), I32),
            pltpu.VMEM((1, 1), I32),
            pltpu.VMEM((ROWS, 2 * NF), BF),
            pltpu.VMEM((CHIPS, 16, ROWS), BF),
            pltpu.VMEM((8, 128), I32),
            pltpu.VMEM((CHIPS, 16, ROWS), BF),
            pltpu.VMEM((1024, 128), I32),
            pltpu.VMEM((4, 2, 16, 16, 512), BF),
            pltpu.VMEM((4, 16, 16, 512), BF),
            pltpu.VMEM((HALF, 16, 256), BF),
            pltpu.VMEM((HALF, 8, 128), I32),
            pltpu.VMEM((HALF, 144, 128), F32),
            pltpu.VMEM((8, 1024, 128), F32),
            pltpu.VMEM((2, 1024, 1024), BF),
            pltpu.VMEM((2, 512, 1024), BF),
            pltpu.VMEM((512, 1024), BF),
            pltpu.VMEM((512, 1024), BF),
            dma, dma((4,)), dma, dma, dma((2,)), dma, dma, dma((4,)), dma((4,)),
            dma((4,)), dma((4,)), dma((5,)), dma((4,)),
        ],
        compiler_params=pltpu.CompilerParams(
            collective_id=0, has_side_effects=True, vmem_limit_bytes=62 << 20
        ),
    )(offset, mid, count, traces, table)


def mix_kernel(own_ref, other_ref, op_ref, out_ref):
    core = lax.axis_index("kx")
    lower = lax.broadcasted_iota(I32, (128, 128), 1) < HALF
    for f in range(FREQS):
        re = op_ref[f, 0]
        im = op_ref[f, 1]
        re_turned, im_turned = pltpu.roll(re, HALF, axis=1), pltpu.roll(im, HALF, axis=1)
        first = core == 0
        re, re_turned = jnp.where(first, re, re_turned), jnp.where(first, re_turned, re)
        im, im_turned = jnp.where(first, im, im_turned), jnp.where(first, im_turned, im)
        by_own = jnp.concatenate(
            [jnp.where(lower, re, -im_turned), jnp.where(lower, im, re_turned)], axis=0
        )
        by_other = jnp.concatenate(
            [jnp.where(lower, re_turned, -im), jnp.where(lower, im_turned, re)], axis=0
        )
        lanes = slice(f * 128, f * 128 + 128)
        z = jnp.concatenate([own_ref[:, lanes], other_ref[:, lanes]], axis=1)
        res = nt(z, jnp.concatenate([by_own, by_other], axis=1))
        out_ref[0, f] = res[:, :128]
        out_ref[1, f] = res[:, 128:]


def mix(own, other, op):
    return pl.pallas_call(
        mix_kernel,
        out_shape=jax.ShapeDtypeStruct((2, 8, 512, 128), F32),
        grid=(8 // FREQS,),
        in_specs=[
            pl.BlockSpec((512, FREQS * 128), lambda f: (0, f)),
            pl.BlockSpec((512, FREQS * 128), lambda f: (0, f)),
            pl.BlockSpec((FREQS, 2, 128, 128), lambda f: (f, 0, 0, 0)),
        ],
        out_specs=pl.BlockSpec((2, FREQS, 512, 128), lambda f: (0, f, 0, 0)),
        compiler_params=pltpu.CompilerParams(vmem_limit_bytes=62 << 20),
    )(own, other, op)


def shards(traces, trace_offset, trace_midpoint, trace_count, operator, table):
    own, other = spectra(
        trace_offset[None, :], trace_midpoint[None, :], trace_count[None, :], traces, table
    )
    return mix(own, other, operator)


def solution(mesh):
    def run(traces, trace_offset, trace_midpoint, trace_count, operator):
        table = jnp.asarray(wave_tables(), BF)
        return jax.shard_map(
            shards,
            mesh=mesh,
            in_specs=(
                P(("off", "kx"), None),
                P(("off", "kx")),
                P(("off", "kx")),
                P(("off", "kx")),
                P("off", None, None, None),
                P(),
            ),
            out_specs=P(None, "off", "kx", None),
            check_vma=False,
        )(traces, trace_offset, trace_midpoint, trace_count, operator, table)

    return run
```

```python
import jax
import jax.numpy as jnp
import numpy as np
from jax import lax
from jax.experimental import pallas as pl
from jax.experimental.pallas import tpu as pltpu
from jax.sharding import PartitionSpec as P

NM = 1024
NF = 512
CAP = 8
ROWS = 512
CHIPS = 64
HALF = 64
UNROLL = 32
WIDTH = 256
DFT_UNROLL = 2
AHEAD = 4
FREQS = 4
BF = jnp.bfloat16
F32 = jnp.float32
I32 = jnp.int32
MESH = pl.DeviceIdType.MESH

VMEM_SPEC = pl.BlockSpec(memory_space=pltpu.VMEM)
HBM_SPEC = pl.BlockSpec(memory_space=pltpu.HBM)


def nt(a, b):
    return lax.dot_general(a, b, (((1,), (1,)), ((), ())), preferred_element_type=F32)


def wave_tables():
    k = np.arange(256)
    tables = []
    for residue in range(4):
        m = np.concatenate([h * 512 + np.arange(128) * 4 + residue for h in range(2)])
        angle = (k[:, None] * m[None, :]) % NM * (2.0 * np.pi / NM)
        tables.append(np.concatenate([np.cos(angle), np.sin(angle)], axis=1))
    return np.stack(tables).astype(np.float32)


def shifted(off, r, i):
    z, x, y = off // 16, (off // 4) % 4, off % 4
    dx, dy = i // 4, i % 4
    dz = (r + 8 - dx - dy) % 4
    return ((z + dz) % 4) * 16 + ((x + dx) % 4) * 4 + (y + dy) % 4


def sort_rows(xy, off_ref, mid_ref, cnt_ref, traces_ref, blocks_ref, meta_ref):
    offset, mid = off_ref[...], mid_ref[...]
    t = lax.broadcasted_iota(I32, (1, ROWS), 1)
    live = t < jnp.broadcast_to(cnt_ref[...], (1, ROWS))
    owner = jnp.where(live, (offset // 2) * 2 + mid // 512, 1024)
    key = owner * ROWS + t

    position = jnp.zeros((128, ROWS), I32)
    start = jnp.zeros((128, ROWS), I32)
    for b in range(4):
        lanes = slice(b * 128, b * 128 + 128)
        key_col = jnp.broadcast_to(key[:, lanes], (128, 128)).T[:, :1]
        own_col = jnp.broadcast_to(owner[:, lanes], (128, 128)).T[:, :1]
        position += (key_col < key).astype(I32)
        start += (own_col < owner).astype(I32)
    position = jnp.sum(position, axis=0, keepdims=True)
    rank = position - jnp.sum(start, axis=0, keepdims=True)
    position = jnp.where(live, position, ROWS)
    slot = (owner // 16) * 128 + ((owner % 16 + xy) % 16) * CAP + rank
    slot = jnp.where(live, slot, -1)

    combo = (offset % 2) * 4 + mid % 4 + 1
    low = (mid % 512) // 4
    fields = jnp.concatenate(
        [position % 128, low, combo, jnp.zeros((13, ROWS), I32)], axis=0
    ).astype(F32).astype(BF)
    hot = (lax.broadcasted_iota(I32, (1024, ROWS), 0) == slot).astype(F32).astype(BF)
    coded = nt(fields, hot)
    coded = coded[0:1] * 8.0 + coded[1:2] * 1024.0 + coded[2:3] * 131072.0
    coded = jnp.concatenate([coded[:, c * 128 : c * 128 + 128] for c in range(8)], axis=0)
    before = jnp.sum(
        (owner < lax.broadcasted_iota(I32, (8, ROWS), 0) * 16).astype(F32), axis=1, keepdims=True
    ).astype(I32)
    lane = lax.broadcasted_iota(I32, (8, 128), 1)
    part = before // 128 + (lane < before % 128).astype(I32)
    meta_ref[...] = coded.astype(I32) + part

    place = (lax.broadcasted_iota(I32, (ROWS, ROWS), 0) == position).astype(F32).astype(BF)

    def cut(j, _):
        lanes = pl.multiple_of(j * 128, 128)
        both = []
        for ri in range(2):
            cols = traces_ref[:, pl.ds(ri * NF + lanes, 128)]
            both.append(
                lax.dot_general(cols, place, (((0,), (1,)), ((), ())), preferred_element_type=F32)
            )
        for g in range(16):
            blocks_ref[j * 16 + g] = jnp.concatenate(
                [both[0][g * 8 : g * 8 + 8], both[1][g * 8 : g * 8 + 8]], axis=0
            ).astype(BF)
        return 0

    lax.fori_loop(0, 4, cut, 0)


def regroup(parts, lane_group):
    now = [parts[(-u) % 16] for u in range(16)]
    for b in range(4):
        bit = (lane_group >> b) % 2 == 1
        now = [jnp.where(bit, now[(u - (1 << b)) % 16], now[u]) for u in range(16)]
    return now


def main_kernel(
    off_hbm, mid_hbm, cnt_hbm, traces_hbm, table_hbm, own_ref, other_ref,
    off_ref, mid_ref, cnt_ref, traces_ref, blocks, meta_out, got, meta, ex, dx, y_ref, mm, acc, s32, s16, table, give, own_part,
    send_sem, recv_sem, msend_sem, mrecv_sem, local_sem, mx_send, mx_recv, dx_send, dx_recv,
    sp_send, sp_recv, load_sem, put_sem,
):
    off, core = lax.axis_index("off"), lax.axis_index("kx")
    xy = off % 16
    total = off // 16 + (off // 4) % 4 + off % 4
    me = (total % 4) * 16 + xy
    mate = (off, 1 - core)

    loads = [
        pltpu.make_async_copy(src, dst, load_sem.at[n])
        for n, (src, dst) in enumerate(
            [(off_hbm, off_ref), (mid_hbm, mid_ref), (cnt_hbm, cnt_ref), (traces_hbm, traces_ref), (table_hbm, table)]
        )
    ]
    for load in loads[:4]:
        load.start()
    bar = pltpu.get_barrier_semaphore()

    def greet(n, _):
        peer = shifted(off, n // 16, n % 16)
        pl.semaphore_signal(bar, inc=1, device_id=(peer, core), device_id_type=MESH)
        return 0

    lax.fori_loop(1, CHIPS, greet, 0)
    pl.semaphore_signal(bar, inc=1, device_id=mate, device_id_type=MESH)
    for load in loads[:4]:
        load.wait()
    loads[4].start()

    sort_rows(xy, off_ref, mid_ref, cnt_ref, traces_ref, blocks, meta_out)

    def meta_slot(which, n):
        return meta.at[pl.ds(pl.multiple_of(which * 512 + n * 8, 8), 8)]

    keep = pltpu.make_async_copy(blocks.at[off], got.at[me], local_sem.at[0])
    keep.start()
    keep_meta = pltpu.make_async_copy(meta_out, meta_slot(0, me), local_sem.at[1])
    keep_meta.start()
    pl.semaphore_wait(bar, CHIPS)

    def send_meta(n, _):
        peer = shifted(off, n // 16, n % 16)
        pltpu.make_async_remote_copy(
            meta_out, meta_slot(0, me), msend_sem, mrecv_sem, device_id=(peer, core), device_id_type=MESH
        ).start()
        return 0

    def send_block(n, _):
        peer = shifted(off, n // 16, n % 16)
        pltpu.make_async_remote_copy(
            blocks.at[peer], got.at[me], send_sem, recv_sem.at[n // 16],
            device_id=(peer, core), device_id_type=MESH,
        ).start()
        return 0

    lax.fori_loop(1, CHIPS, send_meta, 0)
    lax.fori_loop(1, AHEAD * 16, send_block, 0)

    def clear(w, _):
        acc[w] = jnp.zeros((144, 128), F32)
        return 0

    lax.fori_loop(0, HALF, clear, 0)

    keep_meta.wait()
    others = meta.at[pl.ds(0, 63 * 8)]
    pltpu.make_async_remote_copy(others, others, msend_sem, mrecv_sem, device_id=mate, device_id_type=MESH).wait()
    pass_meta = pltpu.make_async_remote_copy(
        meta.at[pl.ds(0, 512)], meta.at[pl.ds(512, 512)], mx_send, mx_recv, device_id=mate, device_id_type=MESH
    )
    pass_meta.start()
    pass_meta.wait()

    group16 = lax.broadcasted_iota(I32, (16, 128), 1) // CAP
    group8 = lax.broadcasted_iota(I32, (8, 128), 1) // CAP

    def meta_by_owner(col, _):
        row = core * 4 + col
        parts = [meta[pl.ds(row + s * 8, 8, stride=128), :] for s in range(16)]
        for w, part in enumerate(regroup(parts, group8)):
            mm[col * 16 + w] = part
        return 0

    lax.fori_loop(0, 4, meta_by_owner, 0)

    def exchange(r):
        return pltpu.make_async_remote_copy(
            ex.at[r, 1 - core], dx.at[r], dx_send.at[r], dx_recv.at[r], device_id=mate, device_id_type=MESH
        )

    def take_in(r):
        base = (total + 4 - r) % 4 * 16

        def arrived(n):
            part = got.at[pl.ds(0, n)]
            pltpu.make_async_remote_copy(
                part, part, send_sem, recv_sem.at[r], device_id=mate, device_id_type=MESH
            ).wait_recv()

        @pl.when(r == 0)
        def _():
            keep.wait()
            arrived(15)

        @pl.when(r > 0)
        def _():
            arrived(16)

        @pl.when(r < 4 - AHEAD)
        def _():
            lax.fori_loop((r + AHEAD) * 16, (r + AHEAD + 1) * 16, send_block, 0)

        def expand(s, _):
            n = base + s
            code = meta[pl.ds(pl.multiple_of(n * 8, 8), 8), :]
            index = (code // 8) % 128
            part = code % 8
            x = [got[n, :, i * 128 : i * 128 + 128].astype(F32) for i in range(4)]
            for c in range(8):
                pick = jnp.broadcast_to(part[c : c + 1], (16, 128))
                src = x[min(c, 3)]
                for i in range(min(c, 3) - 1, -1, -1):
                    src = jnp.where(pick == i, x[i], src)
                at = jnp.broadcast_to(index[c : c + 1], (16, 128))
                out = jnp.take_along_axis(src, at, axis=1, mode="promise_in_bounds")
                ex[r, c // 4, s, :, (c % 4) * 128 : (c % 4) * 128 + 128] = out.astype(BF)
            return 0

        lax.fori_loop(0, 16, expand, 0, unroll=8)
        exchange(r).start()

    def one_round(r, last):
        kind = (total + 4 - r) % 4
        exchange(r).wait()

        def by_owner(which, col):
            lanes = pl.ds(pl.multiple_of(col * 128, 128), 128)
            if which == 0:
                parts = [ex[r, core, s, :, lanes] for s in range(16)]
            else:
                parts = [dx[r, s, :, lanes] for s in range(16)]
            for w, part in enumerate(regroup(parts, group16)):
                y_ref[col * 16 + w, :, which * 128 : which * 128 + 128] = part

        def both_cols(col, _):
            by_owner(0, col)
            by_owner(1, col)
            return 0

        lax.fori_loop(0, 4, both_cols, 0)

        def some_owners(g, _):
            row_id = lax.broadcasted_iota(I32, (128, 128), 0).astype(F32).astype(BF)
            one, zero = jnp.ones((), BF), jnp.zeros((), BF)
            for u in range(UNROLL):
                w = g * UNROLL + u
                left, hot = [], []
                for which in range(2):
                    code = mm[w, pl.ds(which * 4 + kind, 1), :]
                    combo = (code // 131072).astype(F32)
                    low = ((code // 1024) % 128).astype(F32)
                    combo = jnp.broadcast_to(combo, (16, 128)).astype(BF)
                    low = jnp.broadcast_to(low, (128, 128)).astype(BF)
                    data = y_ref[w, :, which * 128 : which * 128 + 128]
                    rows = [jnp.where(combo == jnp.asarray(q + 1, BF), data, zero) for q in range(8)]
                    rows.append(jnp.where(combo == row_id[:16] + one, one, zero))
                    left.append(jnp.concatenate(rows, axis=0))
                    hot.append(jnp.where(low == row_id, one, zero))
                cells = nt(jnp.concatenate(left, axis=1), jnp.concatenate(hot, axis=1))
                if not last:
                    acc[w] += cells
                    continue
                cells = acc[w] + cells
                scale = 1.0 / jnp.maximum(cells[128:136], 1.0)
                for q in range(8):
                    o2, residue = q // 4, q % 4
                    mean = cells[q * 16 : q * 16 + 16] * scale[q : q + 1]
                    cells_of = s32.at[residue * 2 + u % 2]
                    row = g * UNROLL + u // 2 * 2 + o2
                    cells_of[pl.ds(row, 8, stride=136), :] = mean[:8]
                    cells_of[pl.ds(64 + row, 8, stride=136), :] = mean[8:]
            return 0

        lax.fori_loop(0, HALF // UNROLL, some_owners, 0)

    def round_of(r, _):
        take_in(r)
        one_round(r - 1, False)
        return 0

    take_in(jnp.int32(0))
    lax.fori_loop(1, 4, round_of, 0)
    one_round(jnp.int32(3), True)
    sent = blocks.at[pl.ds(0, 63)]
    pltpu.make_async_remote_copy(
        sent, sent, send_sem, recv_sem.at[0], device_id=mate, device_id_type=MESH
    ).wait_send()

    loads[4].wait()
    sign = (1 - 2 * core).astype(F32)

    def handing(j):
        lanes = pl.ds(pl.multiple_of(j * WIDTH, WIDTH), WIDTH)
        return pltpu.make_async_remote_copy(
            give.at[:, lanes], other_ref.at[:, lanes], sp_send.at[j], sp_recv.at[j],
            device_id=mate, device_id_type=MESH,
        )

    def putting(j):
        lanes = pl.ds(pl.multiple_of(j * WIDTH, WIDTH), WIDTH)
        return pltpu.make_async_copy(own_part.at[:, lanes], own_ref.at[:, lanes], put_sem.at[j])

    def transform(j, _):
        r0 = pl.multiple_of(j * WIDTH, WIDTH)
        spec = []
        for n in range(4):
            xs = []
            for f in range(WIDTH // 128):
                q0 = pl.multiple_of((j * (WIDTH // 128) + f) * 136, 8)
                re = [s32[2 * n + h, pl.ds(q0, 64), :].astype(BF) for h in range(2)]
                im = [s32[2 * n + h, pl.ds(q0 + 64, 64), :].astype(BF) for h in range(2)]
                xs.append(jnp.concatenate(re + im, axis=1))
                xs.append(jnp.concatenate(im + [-re[0], -re[1]], axis=1))
            spec.append(nt(table[n], jnp.concatenate(xs, axis=0)))
        f0, f1, f2, f3 = spec
        real = lax.broadcasted_iota(I32, (256, 128), 1) < HALF
        odd = (f1 + f3) * sign
        diff = (f1 - f3) * sign
        turned = []
        for f in range(WIDTH // 128):
            part = pltpu.roll(diff[:, f * 128 : f * 128 + 128], HALF, axis=1)
            turned.append(jnp.where(real, part, -part))
        turned = jnp.concatenate(turned, axis=1) if len(turned) > 1 else turned[0]
        lanes = pl.ds(r0, WIDTH)
        give[:256, lanes] = (f0 + f2 - odd).astype(BF)
        give[256:, lanes] = (f0 - f2 - turned).astype(BF)
        handing(j).start()
        own_part[:256, lanes] = (f0 + f2 + odd).astype(BF)
        own_part[256:, lanes] = (f0 - f2 + turned).astype(BF)
        putting(j).start()
        return 0

    lax.fori_loop(0, 1024 // WIDTH, transform, 0, unroll=DFT_UNROLL)

    def handed(j, _):
        putting(j).wait()
        handing(j).wait()
        return 0

    lax.fori_loop(0, 1024 // WIDTH, handed, 0)


def spectra(offset, mid, count, traces, table):
    half = jax.ShapeDtypeStruct((512, 1024), BF)
    dma = pltpu.SemaphoreType.DMA
    return pl.pallas_call(
        main_kernel,
        out_shape=(half, half),
        in_specs=[HBM_SPEC] * 5,
        out_specs=(HBM_SPEC, HBM_SPEC),
        scratch_shapes=[
            pltpu.VMEM((1, ROWS), I32),
            pltpu.VMEM((1, ROWS), I32),
            pltpu.VMEM((1, 1), I32),
            pltpu.VMEM((ROWS, 2 * NF), BF),
            pltpu.VMEM((CHIPS, 16, ROWS), BF),
            pltpu.VMEM((8, 128), I32),
            pltpu.VMEM((CHIPS, 16, ROWS), BF),
            pltpu.VMEM((1024, 128), I32),
            pltpu.VMEM((4, 2, 16, 16, 512), BF),
            pltpu.VMEM((4, 16, 16, 512), BF),
            pltpu.VMEM((HALF, 16, 256), BF),
            pltpu.VMEM((HALF, 8, 128), I32),
            pltpu.VMEM((HALF, 144, 128), F32),
            pltpu.VMEM((8, 1088, 128), F32),
            pltpu.VMEM((4, 1024, 512), BF),
            pltpu.VMEM((4, 256, 512), BF),
            pltpu.VMEM((512, 1024), BF),
            pltpu.VMEM((512, 1024), BF),
            dma, dma((4,)), dma, dma, dma((2,)), dma, dma, dma((4,)), dma((4,)),
            dma((8,)), dma((8,)), dma((5,)), dma((8,)),
        ],
        compiler_params=pltpu.CompilerParams(
            collective_id=0, has_side_effects=True, vmem_limit_bytes=62 << 20
        ),
    )(offset, mid, count, traces, table)


def mix_kernel(own_ref, other_ref, op_ref, out_ref):
    core = lax.axis_index("kx")
    lower = lax.broadcasted_iota(I32, (128, 128), 1) < HALF
    for f in range(FREQS):
        re = op_ref[f, 0]
        im = op_ref[f, 1]
        re_turned, im_turned = pltpu.roll(re, HALF, axis=1), pltpu.roll(im, HALF, axis=1)
        first = core == 0
        re, re_turned = jnp.where(first, re, re_turned), jnp.where(first, re_turned, re)
        im, im_turned = jnp.where(first, im, im_turned), jnp.where(first, im_turned, im)
        by_own = jnp.concatenate(
            [jnp.where(lower, re, -im_turned), jnp.where(lower, im, re_turned)], axis=0
        )
        by_other = jnp.concatenate(
            [jnp.where(lower, re_turned, -im), jnp.where(lower, im_turned, re)], axis=0
        )
        lanes = slice(f * 128, f * 128 + 128)
        z = jnp.concatenate([own_ref[:, lanes], other_ref[:, lanes]], axis=1)
        res = nt(z, jnp.concatenate([by_own, by_other], axis=1))
        out_ref[0, f] = res[:, :128]
        out_ref[1, f] = res[:, 128:]


def mix(own, other, op):
    return pl.pallas_call(
        mix_kernel,
        out_shape=jax.ShapeDtypeStruct((2, 8, 512, 128), F32),
        grid=(8 // FREQS,),
        in_specs=[
            pl.BlockSpec((512, FREQS * 128), lambda f: (0, f)),
            pl.BlockSpec((512, FREQS * 128), lambda f: (0, f)),
            pl.BlockSpec((FREQS, 2, 128, 128), lambda f: (f, 0, 0, 0)),
        ],
        out_specs=pl.BlockSpec((2, FREQS, 512, 128), lambda f: (0, f, 0, 0)),
        compiler_params=pltpu.CompilerParams(vmem_limit_bytes=62 << 20),
    )(own, other, op)


def shards(traces, trace_offset, trace_midpoint, trace_count, operator, table):
    own, other = spectra(
        trace_offset[None, :], trace_midpoint[None, :], trace_count[None, :], traces, table
    )
    return mix(own, other, operator)


def solution(mesh):
    def run(traces, trace_offset, trace_midpoint, trace_count, operator):
        table = jnp.asarray(wave_tables(), BF)
        return jax.shard_map(
            shards,
            mesh=mesh,
            in_specs=(
                P(("off", "kx"), None),
                P(("off", "kx")),
                P(("off", "kx")),
                P(("off", "kx")),
                P("off", None, None, None),
                P(),
            ),
            out_specs=P(None, "off", "kx", None),
            check_vma=False,
        )(traces, trace_offset, trace_midpoint, trace_count, operator, table)

    return run
```

```python
import jax
import jax.numpy as jnp
import numpy as np
from jax import lax
from jax.experimental import pallas as pl
from jax.experimental.pallas import tpu as pltpu
from jax.sharding import PartitionSpec as P

NM = 1024
NF = 512
CAP = 8
ROWS = 512
CHIPS = 64
HALF = 64
UNROLL = 32
WIDTH = 256
DFT_UNROLL = 4
AHEAD = 4
FREQS = 4
BF = jnp.bfloat16
F32 = jnp.float32
I32 = jnp.int32
MESH = pl.DeviceIdType.MESH

VMEM_SPEC = pl.BlockSpec(memory_space=pltpu.VMEM)
HBM_SPEC = pl.BlockSpec(memory_space=pltpu.HBM)


def nt(a, b):
    return lax.dot_general(a, b, (((1,), (1,)), ((), ())), preferred_element_type=F32)


def wave_tables():
    k = np.arange(256)
    tables = []
    for residue in range(4):
        m = np.concatenate([h * 512 + np.arange(128) * 4 + residue for h in range(2)])
        angle = (k[:, None] * m[None, :]) % NM * (2.0 * np.pi / NM)
        tables.append(np.concatenate([np.cos(angle), np.sin(angle)], axis=1))
    return np.stack(tables).astype(np.float32)


def shifted(off, r, i):
    z, x, y = lax.div(off, 16), lax.rem(lax.div(off, 4), 4), lax.rem(off, 4)
    dx, dy = lax.div(i, 4), lax.rem(i, 4)
    return lax.rem(z + r + 8 - dx - dy, 4) * 16 + lax.rem(x + dx, 4) * 4 + lax.rem(y + dy, 4)


def sort_rows(xy, off_ref, mid_ref, cnt_ref, traces_ref, blocks_ref, meta_ref):
    offset, mid = off_ref[...], mid_ref[...]
    t = lax.broadcasted_iota(I32, (1, ROWS), 1)
    live = t < jnp.broadcast_to(cnt_ref[...], (1, ROWS))
    owner = jnp.where(live, (offset // 2) * 2 + mid // 512, 1024)
    key = owner * ROWS + t

    position = jnp.zeros((128, ROWS), I32)
    start = jnp.zeros((128, ROWS), I32)
    for b in range(4):
        lanes = slice(b * 128, b * 128 + 128)
        key_col = jnp.broadcast_to(key[:, lanes], (128, 128)).T[:, :1]
        own_col = jnp.broadcast_to(owner[:, lanes], (128, 128)).T[:, :1]
        position += (key_col < key).astype(I32)
        start += (own_col < owner).astype(I32)
    position = jnp.sum(position, axis=0, keepdims=True)
    rank = position - jnp.sum(start, axis=0, keepdims=True)
    position = jnp.where(live, position, ROWS)
    slot = (owner // 16) * 128 + ((owner % 16 + xy) % 16) * CAP + rank
    slot = jnp.where(live, slot, -1)

    combo = (offset % 2) * 4 + mid % 4 + 1
    low = (mid % 512) // 4
    fields = jnp.concatenate(
        [position % 128, low, combo, jnp.zeros((13, ROWS), I32)], axis=0
    ).astype(F32).astype(BF)
    hot = (lax.broadcasted_iota(I32, (1024, ROWS), 0) == slot).astype(F32).astype(BF)
    coded = nt(fields, hot)
    coded = coded[0:1] * 8.0 + coded[1:2] * 1024.0 + coded[2:3] * 131072.0
    coded = jnp.concatenate([coded[:, c * 128 : c * 128 + 128] for c in range(8)], axis=0)
    before = jnp.sum(
        (owner < lax.broadcasted_iota(I32, (8, ROWS), 0) * 16).astype(F32), axis=1, keepdims=True
    ).astype(I32)
    lane = lax.broadcasted_iota(I32, (8, 128), 1)
    part = before // 128 + (lane < before % 128).astype(I32)
    meta_ref[...] = coded.astype(I32) + part

    place = (lax.broadcasted_iota(I32, (ROWS, ROWS), 0) == position).astype(F32).astype(BF)

    def cut(j, _):
        lanes = pl.multiple_of(j * 128, 128)
        both = []
        for ri in range(2):
            cols = traces_ref[:, pl.ds(ri * NF + lanes, 128)]
            both.append(
                lax.dot_general(cols, place, (((0,), (1,)), ((), ())), preferred_element_type=F32)
            )
        for g in range(16):
            blocks_ref[j * 16 + g] = jnp.concatenate(
                [both[0][g * 8 : g * 8 + 8], both[1][g * 8 : g * 8 + 8]], axis=0
            ).astype(BF)
        return 0

    lax.fori_loop(0, 4, cut, 0)


def regroup(parts, lane_group):
    now = [parts[(-u) % 16] for u in range(16)]
    for b in range(4):
        bit = (lane_group >> b) % 2 == 1
        now = [jnp.where(bit, now[(u - (1 << b)) % 16], now[u]) for u in range(16)]
    return now


def main_kernel(
    off_hbm, mid_hbm, cnt_hbm, traces_hbm, table_hbm, own_ref, other_ref,
    off_ref, mid_ref, cnt_ref, traces_ref, blocks, meta_out, got, meta, ex, dx, y_ref, mm, acc, s32, s16, table, give, own_part,
    send_sem, recv_sem, msend_sem, mrecv_sem, local_sem, mx_send, mx_recv, dx_send, dx_recv,
    sp_send, sp_recv, load_sem, put_sem,
):
    off, core = lax.axis_index("off"), lax.axis_index("kx")
    xy = off % 16
    total = off // 16 + (off // 4) % 4 + off % 4
    me = (total % 4) * 16 + xy
    mate = (off, 1 - core)

    loads = [
        pltpu.make_async_copy(src, dst, load_sem.at[n])
        for n, (src, dst) in enumerate(
            [(off_hbm, off_ref), (mid_hbm, mid_ref), (cnt_hbm, cnt_ref), (traces_hbm, traces_ref), (table_hbm, table)]
        )
    ]
    for load in loads[:4]:
        load.start()
    bar = pltpu.get_barrier_semaphore()

    def greet(n, _):
        peer = shifted(off, lax.div(n, 16), lax.rem(n, 16))
        pl.semaphore_signal(bar, inc=1, device_id=(peer, core), device_id_type=MESH)
        return 0

    lax.fori_loop(1, CHIPS, greet, 0)
    pl.semaphore_signal(bar, inc=1, device_id=mate, device_id_type=MESH)
    for load in loads[:4]:
        load.wait()
    loads[4].start()

    sort_rows(xy, off_ref, mid_ref, cnt_ref, traces_ref, blocks, meta_out)

    def meta_slot(which, n):
        return meta.at[pl.ds(pl.multiple_of(which * 512 + n * 8, 8), 8)]

    keep = pltpu.make_async_copy(blocks.at[off], got.at[me], local_sem.at[0])
    keep.start()
    keep_meta = pltpu.make_async_copy(meta_out, meta_slot(0, me), local_sem.at[1])
    keep_meta.start()
    pl.semaphore_wait(bar, CHIPS)

    def send_meta(n, _):
        peer = shifted(off, lax.div(n, 16), lax.rem(n, 16))
        pltpu.make_async_remote_copy(
            meta_out, meta_slot(0, me), msend_sem, mrecv_sem, device_id=(peer, core), device_id_type=MESH
        ).start()
        return 0

    def send_block(n, _):
        peer = shifted(off, lax.div(n, 16), lax.rem(n, 16))
        pltpu.make_async_remote_copy(
            blocks.at[peer], got.at[me], send_sem, recv_sem.at[lax.div(n, 16)],
            device_id=(peer, core), device_id_type=MESH,
        ).start()
        return 0

    lax.fori_loop(1, CHIPS, send_meta, 0)
    lax.fori_loop(1, AHEAD * 16, send_block, 0)

    def clear(w, _):
        acc[w] = jnp.zeros((144, 128), F32)
        return 0

    lax.fori_loop(0, HALF, clear, 0)

    keep_meta.wait()
    others = meta.at[pl.ds(0, 63 * 8)]
    pltpu.make_async_remote_copy(others, others, msend_sem, mrecv_sem, device_id=mate, device_id_type=MESH).wait()
    pass_meta = pltpu.make_async_remote_copy(
        meta.at[pl.ds(0, 512)], meta.at[pl.ds(512, 512)], mx_send, mx_recv, device_id=mate, device_id_type=MESH
    )
    pass_meta.start()
    pass_meta.wait()

    group16 = lax.broadcasted_iota(I32, (16, 128), 1) // CAP
    group8 = lax.broadcasted_iota(I32, (8, 128), 1) // CAP

    def meta_by_owner(col, _):
        row = core * 4 + col
        parts = [meta[pl.ds(row + s * 8, 8, stride=128), :] for s in range(16)]
        for w, part in enumerate(regroup(parts, group8)):
            mm[col * 16 + w] = part
        return 0

    lax.fori_loop(0, 4, meta_by_owner, 0)

    def exchange(r):
        return pltpu.make_async_remote_copy(
            ex.at[r, 1 - core], dx.at[r], dx_send.at[r], dx_recv.at[r], device_id=mate, device_id_type=MESH
        )

    def take_in(r):
        base = (total + 4 - r) % 4 * 16

        def arrived(n):
            part = got.at[pl.ds(0, n)]
            pltpu.make_async_remote_copy(
                part, part, send_sem, recv_sem.at[r], device_id=mate, device_id_type=MESH
            ).wait_recv()

        @pl.when(r == 0)
        def _():
            keep.wait()
            arrived(15)

        @pl.when(r > 0)
        def _():
            arrived(16)

        @pl.when(r < 4 - AHEAD)
        def _():
            lax.fori_loop((r + AHEAD) * 16, (r + AHEAD + 1) * 16, send_block, 0)

        def expand(s, _):
            n = base + s
            code = meta[pl.ds(pl.multiple_of(n * 8, 8), 8), :]
            index = (code // 8) % 128
            part = code % 8
            x = [got[n, :, i * 128 : i * 128 + 128].astype(F32) for i in range(4)]
            for c in range(8):
                pick = jnp.broadcast_to(part[c : c + 1], (16, 128))
                src = x[min(c, 3)]
                for i in range(min(c, 3) - 1, -1, -1):
                    src = jnp.where(pick == i, x[i], src)
                at = jnp.broadcast_to(index[c : c + 1], (16, 128))
                out = jnp.take_along_axis(src, at, axis=1, mode="promise_in_bounds")
                ex[r, c // 4, s, :, (c % 4) * 128 : (c % 4) * 128 + 128] = out.astype(BF)
            return 0

        lax.fori_loop(0, 16, expand, 0, unroll=16)
        exchange(r).start()

    def one_round(r, last):
        kind = (total + 4 - r) % 4
        exchange(r).wait()

        def by_owner(which, col):
            lanes = pl.ds(pl.multiple_of(col * 128, 128), 128)
            if which == 0:
                parts = [ex[r, core, s, :, lanes] for s in range(16)]
            else:
                parts = [dx[r, s, :, lanes] for s in range(16)]
            for w, part in enumerate(regroup(parts, group16)):
                y_ref[col * 16 + w, :, which * 128 : which * 128 + 128] = part

        def both_cols(col, _):
            by_owner(0, col)
            by_owner(1, col)
            return 0

        lax.fori_loop(0, 4, both_cols, 0)

        def some_owners(g, _):
            row_id = lax.broadcasted_iota(I32, (128, 128), 0).astype(F32).astype(BF)
            one, zero = jnp.ones((), BF), jnp.zeros((), BF)
            for u in range(UNROLL):
                w = g * UNROLL + u
                left, hot = [], []
                for which in range(2):
                    code = mm[w, pl.ds(which * 4 + kind, 1), :]
                    combo = (code // 131072).astype(F32)
                    low = ((code // 1024) % 128).astype(F32)
                    combo = jnp.broadcast_to(combo, (16, 128)).astype(BF)
                    low = jnp.broadcast_to(low, (128, 128)).astype(BF)
                    data = y_ref[w, :, which * 128 : which * 128 + 128]
                    rows = [jnp.where(combo == jnp.asarray(q + 1, BF), data, zero) for q in range(8)]
                    rows.append(jnp.where(combo == row_id[:16] + one, one, zero))
                    left.append(jnp.concatenate(rows, axis=0))
                    hot.append(jnp.where(low == row_id, one, zero))
                cells = nt(jnp.concatenate(left, axis=1), jnp.concatenate(hot, axis=1))
                if not last:
                    acc[w] += cells
                    continue
                cells = acc[w] + cells
                scale = 1.0 / jnp.maximum(cells[128:136], 1.0)
                for q in range(8):
                    o2, residue = q // 4, q % 4
                    mean = cells[q * 16 : q * 16 + 16] * scale[q : q + 1]
                    cells_of = s32.at[residue * 2 + u % 2]
                    row = g * UNROLL + u // 2 * 2 + o2
                    cells_of[pl.ds(row, 8, stride=136), :] = mean[:8]
                    cells_of[pl.ds(64 + row, 8, stride=136), :] = mean[8:]
            return 0

        lax.fori_loop(0, HALF // UNROLL, some_owners, 0)

    def round_of(r, _):
        take_in(r)
        one_round(r - 1, False)
        return 0

    take_in(jnp.int32(0))
    lax.fori_loop(1, 4, round_of, 0)
    one_round(jnp.int32(3), True)
    sent = blocks.at[pl.ds(0, 63)]
    pltpu.make_async_remote_copy(
        sent, sent, send_sem, recv_sem.at[0], device_id=mate, device_id_type=MESH
    ).wait_send()

    loads[4].wait()
    sign = (1 - 2 * core).astype(F32)

    def handing(j):
        lanes = pl.ds(pl.multiple_of(j * WIDTH, WIDTH), WIDTH)
        return pltpu.make_async_remote_copy(
            give.at[:, lanes], other_ref.at[:, lanes], sp_send.at[j], sp_recv.at[j],
            device_id=mate, device_id_type=MESH,
        )

    def putting(j):
        lanes = pl.ds(pl.multiple_of(j * WIDTH, WIDTH), WIDTH)
        return pltpu.make_async_copy(own_part.at[:, lanes], own_ref.at[:, lanes], put_sem.at[j])

    def transform(j, _):
        r0 = pl.multiple_of(j * WIDTH, WIDTH)
        spec = []
        for n in range(4):
            xs = []
            for f in range(WIDTH // 128):
                q0 = pl.multiple_of((j * (WIDTH // 128) + f) * 136, 8)
                re = [s32[2 * n + h, pl.ds(q0, 64), :].astype(BF) for h in range(2)]
                im = [s32[2 * n + h, pl.ds(q0 + 64, 64), :].astype(BF) for h in range(2)]
                xs.append(jnp.concatenate(re + im, axis=1))
                xs.append(jnp.concatenate(im + [-re[0], -re[1]], axis=1))
            spec.append(nt(table[n], jnp.concatenate(xs, axis=0)))
        f0, f1, f2, f3 = spec
        real = lax.broadcasted_iota(I32, (256, 128), 1) < HALF
        odd = (f1 + f3) * sign
        diff = (f1 - f3) * sign
        turned = []
        for f in range(WIDTH // 128):
            part = pltpu.roll(diff[:, f * 128 : f * 128 + 128], HALF, axis=1)
            turned.append(jnp.where(real, part, -part))
        turned = jnp.concatenate(turned, axis=1) if len(turned) > 1 else turned[0]
        lanes = pl.ds(r0, WIDTH)
        give[:256, lanes] = (f0 + f2 - odd).astype(BF)
        give[256:, lanes] = (f0 - f2 - turned).astype(BF)
        handing(j).start()
        own_part[:256, lanes] = (f0 + f2 + odd).astype(BF)
        own_part[256:, lanes] = (f0 - f2 + turned).astype(BF)
        putting(j).start()
        return 0

    lax.fori_loop(0, 1024 // WIDTH, transform, 0, unroll=DFT_UNROLL)

    def handed(j, _):
        putting(j).wait()
        handing(j).wait()
        return 0

    lax.fori_loop(0, 1024 // WIDTH, handed, 0)


def spectra(offset, mid, count, traces, table):
    half = jax.ShapeDtypeStruct((512, 1024), BF)
    dma = pltpu.SemaphoreType.DMA
    return pl.pallas_call(
        main_kernel,
        out_shape=(half, half),
        in_specs=[HBM_SPEC] * 5,
        out_specs=(HBM_SPEC, HBM_SPEC),
        scratch_shapes=[
            pltpu.VMEM((1, ROWS), I32),
            pltpu.VMEM((1, ROWS), I32),
            pltpu.VMEM((1, 1), I32),
            pltpu.VMEM((ROWS, 2 * NF), BF),
            pltpu.VMEM((CHIPS, 16, ROWS), BF),
            pltpu.VMEM((8, 128), I32),
            pltpu.VMEM((CHIPS, 16, ROWS), BF),
            pltpu.VMEM((1024, 128), I32),
            pltpu.VMEM((4, 2, 16, 16, 512), BF),
            pltpu.VMEM((4, 16, 16, 512), BF),
            pltpu.VMEM((HALF, 16, 256), BF),
            pltpu.VMEM((HALF, 8, 128), I32),
            pltpu.VMEM((HALF, 144, 128), F32),
            pltpu.VMEM((8, 1088, 128), F32),
            pltpu.VMEM((4, 1024, 512), BF),
            pltpu.VMEM((4, 256, 512), BF),
            pltpu.VMEM((512, 1024), BF),
            pltpu.VMEM((512, 1024), BF),
            dma, dma((4,)), dma, dma, dma((2,)), dma, dma, dma((4,)), dma((4,)),
            dma((8,)), dma((8,)), dma((5,)), dma((8,)),
        ],
        compiler_params=pltpu.CompilerParams(
            collective_id=0, has_side_effects=True, vmem_limit_bytes=62 << 20
        ),
    )(offset, mid, count, traces, table)


def mix_kernel(own_ref, other_ref, op_ref, out_ref):
    core = lax.axis_index("kx")
    lower = lax.broadcasted_iota(I32, (128, 128), 1) < HALF
    for f in range(FREQS):
        re = op_ref[f, 0]
        im = op_ref[f, 1]
        re_turned, im_turned = pltpu.roll(re, HALF, axis=1), pltpu.roll(im, HALF, axis=1)
        first = core == 0
        re, re_turned = jnp.where(first, re, re_turned), jnp.where(first, re_turned, re)
        im, im_turned = jnp.where(first, im, im_turned), jnp.where(first, im_turned, im)
        by_own = jnp.concatenate(
            [jnp.where(lower, re, -im_turned), jnp.where(lower, im, re_turned)], axis=0
        )
        by_other = jnp.concatenate(
            [jnp.where(lower, re_turned, -im), jnp.where(lower, im_turned, re)], axis=0
        )
        lanes = slice(f * 128, f * 128 + 128)
        z = jnp.concatenate([own_ref[:, lanes], other_ref[:, lanes]], axis=1)
        res = nt(z, jnp.concatenate([by_own, by_other], axis=1))
        out_ref[0, f] = res[:, :128]
        out_ref[1, f] = res[:, 128:]


def mix(own, other, op):
    return pl.pallas_call(
        mix_kernel,
        out_shape=jax.ShapeDtypeStruct((2, 8, 512, 128), F32),
        grid=(8 // FREQS,),
        in_specs=[
            pl.BlockSpec((512, FREQS * 128), lambda f: (0, f)),
            pl.BlockSpec((512, FREQS * 128), lambda f: (0, f)),
            pl.BlockSpec((FREQS, 2, 128, 128), lambda f: (f, 0, 0, 0)),
        ],
        out_specs=pl.BlockSpec((2, FREQS, 512, 128), lambda f: (0, f, 0, 0)),
        compiler_params=pltpu.CompilerParams(vmem_limit_bytes=62 << 20),
    )(own, other, op)


def shards(traces, trace_offset, trace_midpoint, trace_count, operator, table):
    own, other = spectra(
        trace_offset[None, :], trace_midpoint[None, :], trace_count[None, :], traces, table
    )
    return mix(own, other, operator)


def solution(mesh):
    def run(traces, trace_offset, trace_midpoint, trace_count, operator):
        table = jnp.asarray(wave_tables(), BF)
        return jax.shard_map(
            shards,
            mesh=mesh,
            in_specs=(
                P(("off", "kx"), None),
                P(("off", "kx")),
                P(("off", "kx")),
                P(("off", "kx")),
                P("off", None, None, None),
                P(),
            ),
            out_specs=P(None, "off", "kx", None),
            check_vma=False,
        )(traces, trace_offset, trace_midpoint, trace_count, operator, table)

    return run
```

```python
import jax
import jax.numpy as jnp
import numpy as np
from jax import lax
from jax.experimental import pallas as pl
from jax.experimental.pallas import tpu as pltpu
from jax.sharding import PartitionSpec as P

NM = 1024
NF = 512
CAP = 8
ROWS = 512
CHIPS = 64
HALF = 64
UNROLL = 32
WIDTH = 256
DFT_UNROLL = 4
AHEAD = 4
FREQS = 4
BF = jnp.bfloat16
F32 = jnp.float32
I32 = jnp.int32
MESH = pl.DeviceIdType.MESH

VMEM_SPEC = pl.BlockSpec(memory_space=pltpu.VMEM)
HBM_SPEC = pl.BlockSpec(memory_space=pltpu.HBM)


def nt(a, b):
    return lax.dot_general(a, b, (((1,), (1,)), ((), ())), preferred_element_type=F32)


def wave_tables():
    k = np.arange(256)
    tables = []
    for residue in range(4):
        m = np.concatenate([h * 512 + np.arange(128) * 4 + residue for h in range(2)])
        angle = (k[:, None] * m[None, :]) % NM * (2.0 * np.pi / NM)
        tables.append(np.concatenate([np.cos(angle), np.sin(angle)], axis=1))
    return np.stack(tables).astype(np.float32)


def shifted(off, r, i):
    z, x, y = lax.div(off, 16), lax.rem(lax.div(off, 4), 4), lax.rem(off, 4)
    dx, dy = lax.div(i, 4), lax.rem(i, 4)
    return lax.rem(z + r + 8 - dx - dy, 4) * 16 + lax.rem(x + dx, 4) * 4 + lax.rem(y + dy, 4)


def sort_rows(xy, off_ref, mid_ref, cnt_ref, traces_ref, blocks_ref, meta_ref, planned):
    offset, mid = off_ref[...], mid_ref[...]
    t = lax.broadcasted_iota(I32, (1, ROWS), 1)
    live = t < jnp.broadcast_to(cnt_ref[...], (1, ROWS))
    owner = jnp.where(live, (offset // 2) * 2 + mid // 512, 1024)
    key = owner * ROWS + t

    position = jnp.zeros((128, ROWS), I32)
    start = jnp.zeros((128, ROWS), I32)
    for b in range(4):
        lanes = slice(b * 128, b * 128 + 128)
        key_col = jnp.broadcast_to(key[:, lanes], (128, 128)).T[:, :1]
        own_col = jnp.broadcast_to(owner[:, lanes], (128, 128)).T[:, :1]
        position += (key_col < key).astype(I32)
        start += (own_col < owner).astype(I32)
    position = jnp.sum(position, axis=0, keepdims=True)
    rank = position - jnp.sum(start, axis=0, keepdims=True)
    position = jnp.where(live, position, ROWS)
    slot = (owner // 16) * 128 + ((owner % 16 + xy) % 16) * CAP + rank
    slot = jnp.where(live, slot, -1)

    combo = (offset % 2) * 4 + mid % 4 + 1
    low = (mid % 512) // 4
    fields = jnp.concatenate(
        [position % 128, low, combo, jnp.zeros((13, ROWS), I32)], axis=0
    ).astype(F32).astype(BF)
    hot = (lax.broadcasted_iota(I32, (1024, ROWS), 0) == slot).astype(F32).astype(BF)
    coded = nt(fields, hot)
    coded = coded[0:1] * 8.0 + coded[1:2] * 1024.0 + coded[2:3] * 131072.0
    coded = jnp.concatenate([coded[:, c * 128 : c * 128 + 128] for c in range(8)], axis=0)
    before = jnp.sum(
        (owner < lax.broadcasted_iota(I32, (8, ROWS), 0) * 16).astype(F32), axis=1, keepdims=True
    ).astype(I32)
    lane = lax.broadcasted_iota(I32, (8, 128), 1)
    part = before // 128 + (lane < before % 128).astype(I32)
    meta_ref[...] = coded.astype(I32) + part

    place = (lax.broadcasted_iota(I32, (ROWS, ROWS), 0) == position).astype(F32).astype(BF)

    planned()

    def cut(j, _):
        lanes = pl.multiple_of(j * 128, 128)
        both = []
        for ri in range(2):
            cols = traces_ref[:, pl.ds(ri * NF + lanes, 128)]
            both.append(
                lax.dot_general(cols, place, (((0,), (1,)), ((), ())), preferred_element_type=F32)
            )
        for g in range(16):
            blocks_ref[j * 16 + g] = jnp.concatenate(
                [both[0][g * 8 : g * 8 + 8], both[1][g * 8 : g * 8 + 8]], axis=0
            ).astype(BF)
        return 0

    lax.fori_loop(0, 4, cut, 0)


def regroup(parts, lane_group):
    now = [parts[(-u) % 16] for u in range(16)]
    for b in range(4):
        bit = (lane_group >> b) % 2 == 1
        now = [jnp.where(bit, now[(u - (1 << b)) % 16], now[u]) for u in range(16)]
    return now


def main_kernel(
    off_hbm, mid_hbm, cnt_hbm, traces_hbm, table_hbm, own_ref, other_ref,
    off_ref, mid_ref, cnt_ref, traces_ref, blocks, meta_out, got, meta, ex, dx, y_ref, mm, acc, s32, s16, table, give, own_part,
    send_sem, recv_sem, msend_sem, mrecv_sem, local_sem, mx_send, mx_recv, dx_send, dx_recv,
    sp_send, sp_recv, load_sem, put_sem,
):
    off, core = lax.axis_index("off"), lax.axis_index("kx")
    xy = off % 16
    total = off // 16 + (off // 4) % 4 + off % 4
    me = (total % 4) * 16 + xy
    mate = (off, 1 - core)

    loads = [
        pltpu.make_async_copy(src, dst, load_sem.at[n])
        for n, (src, dst) in enumerate(
            [(off_hbm, off_ref), (mid_hbm, mid_ref), (cnt_hbm, cnt_ref), (traces_hbm, traces_ref), (table_hbm, table)]
        )
    ]
    for load in loads[:4]:
        load.start()
    bar = pltpu.get_barrier_semaphore()

    def greet(n, _):
        peer = shifted(off, lax.div(n, 16), lax.rem(n, 16))
        pl.semaphore_signal(bar, inc=1, device_id=(peer, core), device_id_type=MESH)
        return 0

    lax.fori_loop(1, CHIPS, greet, 0)
    pl.semaphore_signal(bar, inc=1, device_id=mate, device_id_type=MESH)
    for load in loads[:4]:
        load.wait()
    loads[4].start()

    def meta_slot(which, n):
        return meta.at[pl.ds(pl.multiple_of(which * 512 + n * 8, 8), 8)]

    keep_meta = pltpu.make_async_copy(meta_out, meta_slot(0, me), local_sem.at[1])

    def send_meta(n, _):
        peer = shifted(off, lax.div(n, 16), lax.rem(n, 16))
        pltpu.make_async_remote_copy(
            meta_out, meta_slot(0, me), msend_sem, mrecv_sem, device_id=(peer, core), device_id_type=MESH
        ).start()
        return 0

    def send_block(n, _):
        peer = shifted(off, lax.div(n, 16), lax.rem(n, 16))
        pltpu.make_async_remote_copy(
            blocks.at[peer], got.at[me], send_sem, recv_sem.at[lax.div(n, 16)],
            device_id=(peer, core), device_id_type=MESH,
        ).start()
        return 0

    def planned():
        keep_meta.start()
        pl.semaphore_wait(bar, CHIPS)
        lax.fori_loop(1, CHIPS, send_meta, 0)

    sort_rows(xy, off_ref, mid_ref, cnt_ref, traces_ref, blocks, meta_out, planned)
    keep = pltpu.make_async_copy(blocks.at[off], got.at[me], local_sem.at[0])
    keep.start()
    lax.fori_loop(1, CHIPS, send_block, 0)

    def clear(w, _):
        acc[w] = jnp.zeros((144, 128), F32)
        return 0

    lax.fori_loop(0, HALF, clear, 0)

    keep_meta.wait()
    others = meta.at[pl.ds(0, 63 * 8)]
    pltpu.make_async_remote_copy(others, others, msend_sem, mrecv_sem, device_id=mate, device_id_type=MESH).wait()
    pass_meta = pltpu.make_async_remote_copy(
        meta.at[pl.ds(0, 512)], meta.at[pl.ds(512, 512)], mx_send, mx_recv, device_id=mate, device_id_type=MESH
    )
    pass_meta.start()
    pass_meta.wait()

    group16 = lax.broadcasted_iota(I32, (16, 128), 1) // CAP
    group8 = lax.broadcasted_iota(I32, (8, 128), 1) // CAP

    def meta_by_owner(col, _):
        row = core * 4 + col
        parts = [meta[pl.ds(row + s * 8, 8, stride=128), :] for s in range(16)]
        for w, part in enumerate(regroup(parts, group8)):
            mm[col * 16 + w] = part
        return 0

    lax.fori_loop(0, 4, meta_by_owner, 0)

    def exchange(r):
        return pltpu.make_async_remote_copy(
            ex.at[r, 1 - core], dx.at[r], dx_send.at[r], dx_recv.at[r], device_id=mate, device_id_type=MESH
        )

    def take_in(r):
        base = (total + 4 - r) % 4 * 16

        def arrived(n):
            part = got.at[pl.ds(0, n)]
            pltpu.make_async_remote_copy(
                part, part, send_sem, recv_sem.at[r], device_id=mate, device_id_type=MESH
            ).wait_recv()

        @pl.when(r == 0)
        def _():
            keep.wait()
            arrived(15)

        @pl.when(r > 0)
        def _():
            arrived(16)

        @pl.when(r < 4 - AHEAD)
        def _():
            lax.fori_loop((r + AHEAD) * 16, (r + AHEAD + 1) * 16, send_block, 0)

        def expand(s, _):
            n = base + s
            code = meta[pl.ds(pl.multiple_of(n * 8, 8), 8), :]
            index = (code // 8) % 128
            part = code % 8
            x = [got[n, :, i * 128 : i * 128 + 128].astype(F32) for i in range(4)]
            for c in range(8):
                pick = jnp.broadcast_to(part[c : c + 1], (16, 128))
                src = x[min(c, 3)]
                for i in range(min(c, 3) - 1, -1, -1):
                    src = jnp.where(pick == i, x[i], src)
                at = jnp.broadcast_to(index[c : c + 1], (16, 128))
                out = jnp.take_along_axis(src, at, axis=1, mode="promise_in_bounds")
                ex[r, c // 4, s, :, (c % 4) * 128 : (c % 4) * 128 + 128] = out.astype(BF)
            return 0

        lax.fori_loop(0, 16, expand, 0, unroll=16)
        exchange(r).start()

    def one_round(r, last):
        kind = (total + 4 - r) % 4
        exchange(r).wait()

        def by_owner(which, col):
            lanes = pl.ds(pl.multiple_of(col * 128, 128), 128)
            if which == 0:
                parts = [ex[r, core, s, :, lanes] for s in range(16)]
            else:
                parts = [dx[r, s, :, lanes] for s in range(16)]
            for w, part in enumerate(regroup(parts, group16)):
                y_ref[col * 16 + w, :, which * 128 : which * 128 + 128] = part

        def both_cols(col, _):
            by_owner(0, col)
            by_owner(1, col)
            return 0

        lax.fori_loop(0, 4, both_cols, 0)

        def some_owners(g, _):
            row_id = lax.broadcasted_iota(I32, (128, 128), 0).astype(F32).astype(BF)
            one, zero = jnp.ones((), BF), jnp.zeros((), BF)
            for u in range(UNROLL):
                w = g * UNROLL + u
                left, hot = [], []
                for which in range(2):
                    code = mm[w, pl.ds(which * 4 + kind, 1), :]
                    combo = (code // 131072).astype(F32)
                    low = ((code // 1024) % 128).astype(F32)
                    combo = jnp.broadcast_to(combo, (16, 128)).astype(BF)
                    low = jnp.broadcast_to(low, (128, 128)).astype(BF)
                    data = y_ref[w, :, which * 128 : which * 128 + 128]
                    rows = [jnp.where(combo == jnp.asarray(q + 1, BF), data, zero) for q in range(8)]
                    rows.append(jnp.where(combo == row_id[:16] + one, one, zero))
                    left.append(jnp.concatenate(rows, axis=0))
                    hot.append(jnp.where(low == row_id, one, zero))
                cells = nt(jnp.concatenate(left, axis=1), jnp.concatenate(hot, axis=1))
                if not last:
                    acc[w] += cells
                    continue
                cells = acc[w] + cells
                scale = 1.0 / jnp.maximum(cells[128:136], 1.0)
                for q in range(8):
                    o2, residue = q // 4, q % 4
                    mean = cells[q * 16 : q * 16 + 16] * scale[q : q + 1]
                    cells_of = s32.at[residue * 2 + u % 2]
                    row = g * UNROLL + u // 2 * 2 + o2
                    cells_of[pl.ds(row, 8, stride=136), :] = mean[:8]
                    cells_of[pl.ds(64 + row, 8, stride=136), :] = mean[8:]
            return 0

        lax.fori_loop(0, HALF // UNROLL, some_owners, 0)

    def round_of(r, _):
        take_in(r)
        one_round(r - 1, False)
        return 0

    take_in(jnp.int32(0))
    lax.fori_loop(1, 4, round_of, 0)
    one_round(jnp.int32(3), True)
    sent = blocks.at[pl.ds(0, 63)]
    pltpu.make_async_remote_copy(
        sent, sent, send_sem, recv_sem.at[0], device_id=mate, device_id_type=MESH
    ).wait_send()

    loads[4].wait()
    sign = (1 - 2 * core).astype(F32)

    def handing(j):
        lanes = pl.ds(pl.multiple_of(j * WIDTH, WIDTH), WIDTH)
        return pltpu.make_async_remote_copy(
            give.at[:, lanes], other_ref.at[:, lanes], sp_send.at[j], sp_recv.at[j],
            device_id=mate, device_id_type=MESH,
        )

    def putting(j):
        lanes = pl.ds(pl.multiple_of(j * WIDTH, WIDTH), WIDTH)
        return pltpu.make_async_copy(own_part.at[:, lanes], own_ref.at[:, lanes], put_sem.at[j])

    def transform(j, _):
        r0 = pl.multiple_of(j * WIDTH, WIDTH)
        spec = []
        for n in range(4):
            xs = []
            for f in range(WIDTH // 128):
                q0 = pl.multiple_of((j * (WIDTH // 128) + f) * 136, 8)
                re = [s32[2 * n + h, pl.ds(q0, 64), :].astype(BF) for h in range(2)]
                im = [s32[2 * n + h, pl.ds(q0 + 64, 64), :].astype(BF) for h in range(2)]
                xs.append(jnp.concatenate(re + im, axis=1))
                xs.append(jnp.concatenate(im + [-re[0], -re[1]], axis=1))
            spec.append(nt(table[n], jnp.concatenate(xs, axis=0)))
        f0, f1, f2, f3 = spec
        real = lax.broadcasted_iota(I32, (256, 128), 1) < HALF
        odd = (f1 + f3) * sign
        diff = (f1 - f3) * sign
        turned = []
        for f in range(WIDTH // 128):
            part = pltpu.roll(diff[:, f * 128 : f * 128 + 128], HALF, axis=1)
            turned.append(jnp.where(real, part, -part))
        turned = jnp.concatenate(turned, axis=1) if len(turned) > 1 else turned[0]
        lanes = pl.ds(r0, WIDTH)
        give[:256, lanes] = (f0 + f2 - odd).astype(BF)
        give[256:, lanes] = (f0 - f2 - turned).astype(BF)
        handing(j).start()
        own_part[:256, lanes] = (f0 + f2 + odd).astype(BF)
        own_part[256:, lanes] = (f0 - f2 + turned).astype(BF)
        putting(j).start()
        return 0

    lax.fori_loop(0, 1024 // WIDTH, transform, 0, unroll=DFT_UNROLL)

    def handed(j, _):
        putting(j).wait()
        handing(j).wait()
        return 0

    lax.fori_loop(0, 1024 // WIDTH, handed, 0)


def spectra(offset, mid, count, traces, table):
    half = jax.ShapeDtypeStruct((512, 1024), BF)
    dma = pltpu.SemaphoreType.DMA
    return pl.pallas_call(
        main_kernel,
        out_shape=(half, half),
        in_specs=[HBM_SPEC] * 5,
        out_specs=(HBM_SPEC, HBM_SPEC),
        scratch_shapes=[
            pltpu.VMEM((1, ROWS), I32),
            pltpu.VMEM((1, ROWS), I32),
            pltpu.VMEM((1, 1), I32),
            pltpu.VMEM((ROWS, 2 * NF), BF),
            pltpu.VMEM((CHIPS, 16, ROWS), BF),
            pltpu.VMEM((8, 128), I32),
            pltpu.VMEM((CHIPS, 16, ROWS), BF),
            pltpu.VMEM((1024, 128), I32),
            pltpu.VMEM((4, 2, 16, 16, 512), BF),
            pltpu.VMEM((4, 16, 16, 512), BF),
            pltpu.VMEM((HALF, 16, 256), BF),
            pltpu.VMEM((HALF, 8, 128), I32),
            pltpu.VMEM((HALF, 144, 128), F32),
            pltpu.VMEM((8, 1088, 128), F32),
            pltpu.VMEM((4, 1024, 512), BF),
            pltpu.VMEM((4, 256, 512), BF),
            pltpu.VMEM((512, 1024), BF),
            pltpu.VMEM((512, 1024), BF),
            dma, dma((4,)), dma, dma, dma((2,)), dma, dma, dma((4,)), dma((4,)),
            dma((8,)), dma((8,)), dma((5,)), dma((8,)),
        ],
        compiler_params=pltpu.CompilerParams(
            collective_id=0, has_side_effects=True, vmem_limit_bytes=62 << 20
        ),
    )(offset, mid, count, traces, table)


def mix_kernel(own_ref, other_ref, op_ref, out_ref):
    core = lax.axis_index("kx")
    lower = lax.broadcasted_iota(I32, (128, 128), 1) < HALF
    for f in range(FREQS):
        re = op_ref[f, 0]
        im = op_ref[f, 1]
        re_turned, im_turned = pltpu.roll(re, HALF, axis=1), pltpu.roll(im, HALF, axis=1)
        first = core == 0
        re, re_turned = jnp.where(first, re, re_turned), jnp.where(first, re_turned, re)
        im, im_turned = jnp.where(first, im, im_turned), jnp.where(first, im_turned, im)
        by_own = jnp.concatenate(
            [jnp.where(lower, re, -im_turned), jnp.where(lower, im, re_turned)], axis=0
        )
        by_other = jnp.concatenate(
            [jnp.where(lower, re_turned, -im), jnp.where(lower, im_turned, re)], axis=0
        )
        lanes = slice(f * 128, f * 128 + 128)
        z = jnp.concatenate([own_ref[:, lanes], other_ref[:, lanes]], axis=1)
        res = nt(z, jnp.concatenate([by_own, by_other], axis=1))
        out_ref[0, f] = res[:, :128]
        out_ref[1, f] = res[:, 128:]


def mix(own, other, op):
    return pl.pallas_call(
        mix_kernel,
        out_shape=jax.ShapeDtypeStruct((2, 8, 512, 128), F32),
        grid=(8 // FREQS,),
        in_specs=[
            pl.BlockSpec((512, FREQS * 128), lambda f: (0, f)),
            pl.BlockSpec((512, FREQS * 128), lambda f: (0, f)),
            pl.BlockSpec((FREQS, 2, 128, 128), lambda f: (f, 0, 0, 0)),
        ],
        out_specs=pl.BlockSpec((2, FREQS, 512, 128), lambda f: (0, f, 0, 0)),
        compiler_params=pltpu.CompilerParams(vmem_limit_bytes=62 << 20),
    )(own, other, op)


def shards(traces, trace_offset, trace_midpoint, trace_count, operator, table):
    own, other = spectra(
        trace_offset[None, :], trace_midpoint[None, :], trace_count[None, :], traces, table
    )
    return mix(own, other, operator)


def solution(mesh):
    def run(traces, trace_offset, trace_midpoint, trace_count, operator):
        table = jnp.asarray(wave_tables(), BF)
        return jax.shard_map(
            shards,
            mesh=mesh,
            in_specs=(
                P(("off", "kx"), None),
                P(("off", "kx")),
                P(("off", "kx")),
                P(("off", "kx")),
                P("off", None, None, None),
                P(),
            ),
            out_specs=P(None, "off", "kx", None),
            check_vma=False,
        )(traces, trace_offset, trace_midpoint, trace_count, operator, table)

    return run
```
